32 devices in a mesh: grp: 2 (over y), dom: 4 (over z), st: 2 (over x), sub: 2 (over core).
Axes of the slice: x: 2, y: 2, z: 4, core: 2. Of those that a mesh axis runs over, the one named last changes fastest.
Arguments:
- node_feats: bfloat16 [256, 256], P(('grp', 'dom')), parts along dimension 0, may hold values from -6 to 6
- distance: float32 [256, 64], P(('grp', 'dom'), ('st', 'sub')), parts along dimension 0, may hold values from 1.3 to 6.5
- neighbours: int32 [256, 64], P(('grp', 'dom'), ('st', 'sub')), parts along dimension 0, may hold values from 0 to 127, as said below
- counts: int32 [256], P(('grp', 'dom')), parts along dimension 0, may hold values from 16 to 64
- w_source: bfloat16 [256, 256], replicated, may hold values from -0.375 to 0.375
- w_target: bfloat16 [256, 256], replicated, may hold values from -0.375 to 0.375
- w_radial: bfloat16 [128, 256], replicated, may hold values from -0.5 to 0.5
- w_middle: bfloat16 [256, 256], replicated, may hold values from -0.375 to 0.375
- w_output: bfloat16 [256, 169], replicated, may hold values from -0.125 to 0.125
- w_onsite: bfloat16 [256, 169], replicated, may hold values from -0.375 to 0.375
- initial: float32 [256, 13, 128], P(('grp', 'dom')), parts along dimension 0, may hold values from -100 to 100
Outputs:
- alpha_blocks: float32 [4, 128, 128], P('grp'), parts along dimension 0
- beta_blocks: float32 [4, 128, 128], P('grp'), parts along dimension 0
- next_states: float32 [256, 13, 128], P(('grp', 'dom')), parts along dimension 0
The draws below stay inside these ranges and needn't reach their ends.
There are 2 independent parts, one for each index of `grp`. The reference program is written for one: setup_inputs(seed, part) draws one part's arguments, and reference() takes and returns one part's arrays. A program takes and returns all parts, laid end to end along the dimension named above; an argument that names none is the same for every part. Nothing has to cross between parts.
Inputs may be any that keep to these rules, and one draw needn't show every extreme that they name: `neighbours`: every partner lies in the atom's own domain of 32 consecutive atoms (never the atom itself) or in the next domain, the last domain's next being the first.
All inputs are finite; a program needn't handle non-finite values.
Results may differ from the reference program's by a relative error of at most 0.014.
Values may be sent and summed in bfloat16 or wider, within the bound.
No kernel may reach another device: no remote copies, remote signals or barrier semaphores. Data moves between devices by JAX's collectives and lax.ppermute only.
A program may use at most 64 MiB of HBM per device.

```python
import jax
import jax.numpy as jnp
from jax import lax

ORB = 13
FEAT = 256
EDGE_HID = 256
BASIS = 128
STATES = 128
SLOTS = 64
STEPS = 2
ATOMS_DOM = 32
ATOMS = 128
N_DOM = 4


def draw_neighbours(key, part):
    key = jax.random.fold_in(key, 11)
    key_offset, key_partner = jax.random.split(key)
    atom_index = jnp.arange(ATOMS, dtype=jnp.int32)[:, None]
    domain = atom_index // ATOMS_DOM
    position = atom_index % ATOMS_DOM
    offset = jax.random.randint(key_offset, (ATOMS, SLOTS), 0, 2)
    partner = jax.random.randint(key_partner, (ATOMS, SLOTS), 0, ATOMS_DOM)
    partner = jnp.where((offset == 0) & (partner == position), (partner + 1) % ATOMS_DOM, partner)
    return ((domain + offset) * ATOMS_DOM + partner) % ATOMS


def draw_initial(key, part):
    key = jax.random.fold_in(key, 5)
    key_one = jax.random.fold_in(key, 0)
    atom_index = jnp.arange(ATOMS, dtype=jnp.float32)
    domain_ramp = (1.0 + 2.0 * atom_index / ATOMS)[:, None, None]
    return domain_ramp * jnp.clip(jax.random.normal(key_one, (ATOMS, ORB, STATES), jnp.float32), -6.0, 6.0)


def plant(entries, key, smallest, largest):
    longest = entries.shape.index(max(entries.shape))
    spots = []
    for shift in (0, 1):
        where = [jax.random.randint(jax.random.fold_in(key, axis), (), 0, length) for axis, length in enumerate(entries.shape)]
        where[longest] = (where[longest] + shift) % entries.shape[longest]
        spots.append(tuple(where))
    return entries.at[spots[0]].set(smallest).at[spots[1]].set(largest)


def shard_levels(stream_key, dims, pieces, smallest, high):
    factor_of = 1.0
    for dim, blocks in pieces:
        heights = jax.random.uniform(jax.random.fold_in(jax.random.fold_in(stream_key, 6), dim), (blocks,), jnp.float32, smallest / len(pieces), high / len(pieces))
        factor_of = factor_of * jnp.repeat(jnp.exp(heights), dims[dim] // blocks).reshape((-1,) + (1,) * (len(dims) - 1 - dim))
    return factor_of


def bell_draw(stream_key, dims, spread, limit, pieces=(), kind=jnp.bfloat16):
    array = jax.random.normal(stream_key, dims, jnp.float32) * spread
    if len(pieces) > 0:
        array = shard_levels(stream_key, dims, pieces, -0.22, 0.18) * array
    return jnp.clip(array, min=-limit, max=limit).astype(kind)


def setup_inputs(seed: int = 0, part: int = 0) -> dict:
    keys = jax.random.split(jax.random.key(seed), 12)
    own_keys = jax.random.split(jax.random.fold_in(keys[11], part), 12)
    node_feats = bell_draw(own_keys[0], (ATOMS, FEAT), 1.0, 6.0, ((0, 4),))
    distance = jnp.clip(1.3 + 5.2 * jax.random.uniform(own_keys[1], (ATOMS, SLOTS), jnp.float32) ** shard_levels(own_keys[1], (ATOMS, SLOTS), ((0, 4), (1, 4)), -0.2, 0.2), 1.3, 6.5)
    neighbours = draw_neighbours(jax.random.fold_in(jax.random.fold_in(keys[11], part), 71), part)
    counts = plant(jax.random.randint(own_keys[3], (ATOMS,), SLOTS // 4, SLOTS + 1), jax.random.fold_in(own_keys[3], 1), SLOTS // 4, SLOTS).astype(jnp.int32)
    w_source = bell_draw(keys[4], (FEAT, EDGE_HID), FEAT ** -0.5, 0.375)
    w_target = bell_draw(keys[5], (FEAT, EDGE_HID), FEAT ** -0.5, 0.375)
    w_radial = bell_draw(keys[6], (BASIS, EDGE_HID), BASIS ** -0.5, 0.5)
    w_middle = bell_draw(keys[7], (EDGE_HID, EDGE_HID), EDGE_HID ** -0.5, 0.375)
    w_output = bell_draw(keys[8], (EDGE_HID, ORB * ORB), (EDGE_HID * 8) ** -0.5, 0.125)
    w_onsite = bell_draw(keys[9], (FEAT, ORB * ORB), FEAT ** -0.5, 0.375)
    initial = draw_initial(jax.random.fold_in(jax.random.fold_in(keys[11], part), 71), part)
    return dict(node_feats=node_feats, distance=distance, neighbours=neighbours, counts=counts, w_source=w_source, w_target=w_target, w_radial=w_radial, w_middle=w_middle, w_output=w_output, w_onsite=w_onsite, initial=initial)


RADIUS = 7.0

def radial(distance, basis_count):
    centres = RADIUS * jnp.arange(basis_count, dtype=jnp.float32) / basis_count
    spacing = RADIUS / basis_count
    return jnp.exp(-jnp.square((distance[..., None] - centres) / (2.0 * spacing)))

def envelope(distance, usable):
    return 0.5 * (jnp.cos(jnp.pi * distance / RADIUS) + 1.0) * usable.astype(jnp.float32)

def onsite_blocks(node_feats, w_onsite):
    projected = jnp.dot(node_feats, w_onsite, preferred_element_type=jnp.float32)
    matrix = projected.reshape(-1, ORB, ORB)
    return (0.5 * (matrix + jnp.swapaxes(matrix, 1, 2))).astype(jnp.bfloat16)

def pair_blocks(source_rows, target_rows, distance, usable, w_radial, w_middle, w_output):
    radial_basis = radial(distance, w_radial.shape[0]).astype(jnp.bfloat16)
    mixed = source_rows[:, None, :].astype(jnp.float32) + target_rows.astype(jnp.float32)
    mixed = mixed + jnp.dot(radial_basis, w_radial, preferred_element_type=jnp.float32)
    hidden_one = jax.nn.silu(mixed).astype(jnp.bfloat16)
    second = jax.nn.silu(jnp.dot(hidden_one, w_middle, preferred_element_type=jnp.float32)).astype(jnp.bfloat16)
    output_blocks = jnp.dot(second, w_output, preferred_element_type=jnp.float32) * envelope(distance, usable)[..., None]
    return output_blocks.astype(jnp.bfloat16).reshape(distance.shape[0], distance.shape[1], ORB, ORB)

def gram_matrix(left, right, rows_total):
    return jnp.einsum('ris,rit->st', left, right, precision=lax.Precision.HIGHEST) / rows_total

def combine(states, matrix):
    return jnp.einsum('ris,st->rit', states, matrix, precision=lax.Precision.HIGHEST)

def upper_factor(matrix):
    order = matrix.shape[0]
    places = jnp.arange(order, dtype=jnp.int32)

    def column_step(column_index, carry):
        work, lower = carry
        column = lax.dynamic_slice_in_dim(work, column_index, 1, 1)[:, 0]
        pivot = jnp.sqrt(lax.dynamic_slice_in_dim(column, column_index, 1, 0)[0])
        scaled = jnp.where(places >= column_index, column / pivot, jnp.zeros_like(column))
        work = work - scaled[:, None] * scaled[None, :]
        lower = lax.dynamic_update_slice_in_dim(lower, scaled[:, None], column_index, 1)
        return (work, lower)
    work, lower = lax.fori_loop(0, order, column_step, (matrix, jnp.zeros_like(matrix)))
    return lower.T

def upper_inverse(factor):
    order = factor.shape[0]
    identity = jnp.eye(order, dtype=factor.dtype)

    def row_step(counter, inverse):
        row_index = order - 1 - counter
        factor_row = lax.dynamic_slice_in_dim(factor, row_index, 1, 0)
        unit_row = lax.dynamic_slice_in_dim(identity, row_index, 1, 0)
        pivot = lax.dynamic_slice_in_dim(factor_row[0], row_index, 1, 0)[0]
        known = jnp.dot(factor_row, inverse, precision=lax.Precision.HIGHEST)
        fresh = (unit_row - known) / pivot
        return lax.dynamic_update_slice_in_dim(inverse, fresh, row_index, 0)
    return lax.fori_loop(0, order, row_step, jnp.zeros_like(factor))

def divide_right(residue, factor):
    return combine(residue, upper_inverse(factor))

def onsite_apply(onsite, states):
    return jnp.einsum('aij,ajs->ais', onsite, states, precision=lax.Precision.HIGHEST)

def lanczos(states, operate, totals, rows_total):
    factor = upper_factor(totals(gram_matrix(states, states, rows_total)))
    current = divide_right(states, factor)
    previous = current
    beta_prev = factor
    alpha_list = []
    beta_list = []
    for iteration in range(STEPS):
        residue = operate(current)
        if iteration > 0:
            residue = residue - combine(previous, beta_prev.T)
        alpha_block = totals(gram_matrix(current, residue, rows_total))
        residue = residue - combine(current, alpha_block)
        beta_block = upper_factor(totals(gram_matrix(residue, residue, rows_total)))
        previous = current
        current = divide_right(residue, beta_block)
        beta_prev = beta_block
        alpha_list.append(alpha_block)
        beta_list.append(beta_block)
    return (jnp.stack(alpha_list), jnp.stack(beta_list), current)

def reference(node_feats, distance, neighbours, counts, w_source, w_target, w_radial, w_middle, w_output, w_onsite, initial):
    source = jnp.dot(node_feats, w_source, preferred_element_type=jnp.float32).astype(jnp.bfloat16)
    target = jnp.dot(node_feats, w_target, preferred_element_type=jnp.float32).astype(jnp.bfloat16)
    usable = jnp.arange(SLOTS, dtype=jnp.int32)[None, :] < counts[:, None]

    def domain_blocks(domain):
        begin = (domain * ATOMS_DOM).astype(jnp.int32)
        source_rows = lax.dynamic_slice_in_dim(source, begin, ATOMS_DOM, 0)
        index_rows = lax.dynamic_slice_in_dim(neighbours, begin, ATOMS_DOM, 0)
        reach = lax.dynamic_slice_in_dim(distance, begin, ATOMS_DOM, 0)
        usable_rows = lax.dynamic_slice_in_dim(usable, begin, ATOMS_DOM, 0)
        return pair_blocks(source_rows, target[index_rows], reach, usable_rows, w_radial, w_middle, w_output)
    blocks = lax.map(domain_blocks, jnp.arange(N_DOM, dtype=jnp.int32)).reshape(ATOMS, SLOTS, ORB, ORB)
    onsite = onsite_blocks(node_feats, w_onsite).astype(jnp.float32)

    def operate(states):

        def visit_domain(running, domain):
            begin = (domain * ATOMS_DOM).astype(jnp.int32)
            block_rows = lax.dynamic_slice_in_dim(blocks, begin, ATOMS_DOM, 0).astype(jnp.float32)
            index_rows = lax.dynamic_slice_in_dim(neighbours, begin, ATOMS_DOM, 0)
            own_rows = lax.dynamic_slice_in_dim(states, begin, ATOMS_DOM, 0)
            forward = jnp.einsum('akij,akjs->ais', block_rows, states[index_rows], precision=lax.Precision.HIGHEST)
            backward = jnp.einsum('akij,ais->akjs', block_rows, own_rows, precision=lax.Precision.HIGHEST)
            running = running + jax.ops.segment_sum(backward.reshape(-1, ORB, states.shape[-1]), index_rows.reshape(-1), num_segments=ATOMS)
            present = lax.dynamic_slice_in_dim(running, begin, ATOMS_DOM, 0)
            running = lax.dynamic_update_slice_in_dim(running, present + forward, begin, 0)
            return (running, None)
        onsite_terms = onsite_apply(onsite, states)
        result, unused = lax.scan(visit_domain, onsite_terms, jnp.arange(N_DOM, dtype=jnp.int32))
        return result

    def totals(value):
        return value
    return lanczos(initial, operate, totals, float(ATOMS * ORB))
```

```python
import jax
import jax.numpy as jnp
from jax import lax
from jax.experimental import pallas as pl
from jax.experimental.pallas import tpu as pltpu
from jax.sharding import PartitionSpec as P

ORB = 13
STEPS = 2


RADIUS = 7.0


def shifted(shard, axis, by):
    devices = lax.axis_size(axis)
    return lax.ppermute(shard, axis, [(i, (i + by) % devices) for i in range(devices)])


def radial(distance, basis_count):
    centres = RADIUS * jnp.arange(basis_count, dtype=jnp.float32) / basis_count
    spacing = RADIUS / basis_count
    return jnp.exp(-jnp.square((distance[..., None] - centres) / (2.0 * spacing)))


def envelope(distance, usable):
    return 0.5 * (jnp.cos(jnp.pi * distance / RADIUS) + 1.0) * usable.astype(jnp.float32)


def onsite_blocks(node_feats, w_onsite):
    projected = jnp.dot(node_feats, w_onsite, preferred_element_type=jnp.float32)
    matrix = projected.reshape(-1, ORB, ORB)
    return (0.5 * (matrix + jnp.swapaxes(matrix, 1, 2))).astype(jnp.bfloat16)


def pair_blocks(source_rows, target_rows, distance, usable, w_radial, w_middle, w_output):
    radial_basis = radial(distance, w_radial.shape[0]).astype(jnp.bfloat16)
    mixed = source_rows[:, None, :].astype(jnp.float32) + target_rows.astype(jnp.float32)
    mixed = mixed + jnp.dot(radial_basis, w_radial, preferred_element_type=jnp.float32)
    hidden_one = jax.nn.silu(mixed).astype(jnp.bfloat16)
    second = jax.nn.silu(jnp.dot(hidden_one, w_middle, preferred_element_type=jnp.float32)).astype(
        jnp.bfloat16
    )
    output_blocks = (
        jnp.dot(second, w_output, preferred_element_type=jnp.float32)
        * envelope(distance, usable)[..., None]
    )
    return output_blocks.astype(jnp.bfloat16).reshape(
        distance.shape[0], distance.shape[1], ORB, ORB
    )


def gram_matrix(left, right, rows_total):
    return jnp.einsum("ris,rit->st", left, right, precision=lax.Precision.HIGHEST) / rows_total


def combine(states, matrix):
    return jnp.einsum("ris,st->rit", states, matrix, precision=lax.Precision.HIGHEST)


def upper_factor(matrix):
    order = matrix.shape[0]
    places = jnp.arange(order, dtype=jnp.int32)

    def column_step(column_index, carry):
        work, lower = carry
        column = lax.dynamic_slice_in_dim(work, column_index, 1, 1)[:, 0]
        pivot = jnp.sqrt(lax.dynamic_slice_in_dim(column, column_index, 1, 0)[0])
        scaled = jnp.where(places >= column_index, column / pivot, jnp.zeros_like(column))
        work = work - scaled[:, None] * scaled[None, :]
        lower = lax.dynamic_update_slice_in_dim(lower, scaled[:, None], column_index, 1)
        return (work, lower)

    work, lower = lax.fori_loop(0, order, column_step, (matrix, jnp.zeros_like(matrix)))
    return lower.T


def upper_inverse(factor):
    order = factor.shape[0]
    identity = jnp.eye(order, dtype=factor.dtype)

    def row_step(counter, inverse):
        row_index = order - 1 - counter
        factor_row = lax.dynamic_slice_in_dim(factor, row_index, 1, 0)
        unit_row = lax.dynamic_slice_in_dim(identity, row_index, 1, 0)
        pivot = lax.dynamic_slice_in_dim(factor_row[0], row_index, 1, 0)[0]
        known = jnp.dot(factor_row, inverse, precision=lax.Precision.HIGHEST)
        fresh = (unit_row - known) / pivot
        return lax.dynamic_update_slice_in_dim(inverse, fresh, row_index, 0)

    return lax.fori_loop(0, order, row_step, jnp.zeros_like(factor))


def divide_right(residue, factor):
    return combine(residue, upper_inverse(factor))


def onsite_apply(onsite, states):
    return jnp.einsum("aij,ajs->ais", onsite, states, precision=lax.Precision.HIGHEST)


def lanczos(states, operate, totals, rows_total):
    factor = upper_factor(totals(gram_matrix(states, states, rows_total)))
    current = divide_right(states, factor)
    previous = current
    beta_prev = factor
    alpha_list = []
    beta_list = []
    for iteration in range(STEPS):
        residue = operate(current)
        if iteration > 0:
            residue = residue - combine(previous, beta_prev.T)
        alpha_block = totals(gram_matrix(current, residue, rows_total))
        residue = residue - combine(current, alpha_block)
        beta_block = upper_factor(totals(gram_matrix(residue, residue, rows_total)))
        previous = current
        current = divide_right(residue, beta_block)
        beta_prev = beta_block
        alpha_list.append(alpha_block)
        beta_list.append(beta_block)
    return (jnp.stack(alpha_list), jnp.stack(beta_list), current)


def body_spread(
    node_feats,
    distance,
    neighbours,
    counts,
    w_source,
    w_target,
    w_radial,
    w_middle,
    w_output,
    w_onsite,
    initial,
):
    atoms_here = node_feats.shape[0]
    slots_here = neighbours.shape[1]
    domain = lax.axis_index("dom")
    member = lax.axis_index(("st", "sub"))
    atoms_all = atoms_here * lax.axis_size("dom")
    rows_total = float(atoms_all * ORB)
    ghost_feats = shifted(node_feats, "dom", -1)
    local_index = (neighbours - domain * atoms_here) % atoms_all
    source = jnp.dot(node_feats, w_source, preferred_element_type=jnp.float32).astype(jnp.bfloat16)
    combined_feats = jnp.concatenate([node_feats, ghost_feats], axis=0)
    target = jnp.dot(combined_feats, w_target, preferred_element_type=jnp.float32).astype(
        jnp.bfloat16
    )
    slot_index = member * slots_here + jnp.arange(slots_here, dtype=jnp.int32)
    usable = slot_index[None, :] < counts[:, None]
    blocks = pair_blocks(
        source, target[local_index], distance, usable, w_radial, w_middle, w_output
    ).astype(jnp.float32)

    def edge_terms(whole_rows, ghost_rows):
        combined = jnp.concatenate([whole_rows, ghost_rows], axis=0)
        forward = jnp.einsum(
            "akij,akjs->ais", blocks, combined[local_index], precision=lax.Precision.HIGHEST
        )
        backward = jnp.einsum("akij,ais->akjs", blocks, whole_rows, precision=lax.Precision.HIGHEST)
        spread = jax.ops.segment_sum(
            backward.reshape(-1, ORB, whole_rows.shape[-1]),
            local_index.reshape(-1),
            num_segments=2 * atoms_here,
        )
        arrived = shifted(spread[atoms_here:], "dom", 1)
        return forward + spread[:atoms_here] + arrived

    onsite = onsite_blocks(node_feats, w_onsite).astype(jnp.float32)

    def operate(current):
        ghost_rows = shifted(current, "dom", -1)
        summed = lax.psum(edge_terms(current, ghost_rows), ("st", "sub"))
        return summed + onsite_apply(onsite, current)

    def totals(value):
        return lax.psum(value, "dom")

    alpha_blocks, beta_blocks, final_rows = lanczos(initial, operate, totals, rows_total)
    return (alpha_blocks, beta_blocks, final_rows)


F32 = jnp.float32
BF16 = jnp.bfloat16
LANES = 128
PAD = 16
PANEL = 8
VMEM_LIMIT = 56 * 1024 * 1024


def dims(left, right):
    return (((left,), (right,)), ((), ()))


def dot(left, right, contract):
    return lax.dot_general(left, right, contract, preferred_element_type=F32)


def split(value):
    high = value.astype(BF16)
    return high, (value - high.astype(F32)).astype(BF16)


def dot_split(left, right, contract):
    lh, ll = left
    rh, rl = right
    return dot(lh, rh, contract) + (dot(ll, rh, contract) + dot(lh, rl, contract))


NN = dims(1, 0)
NT = dims(1, 1)
TN = dims(0, 0)


def silu(value):
    half = 0.5 * value
    return half + half * jnp.tanh(half)


def spread_rows(value, row, count):
    return jnp.broadcast_to(value[row : row + 1, :], (count, value.shape[1]))


def network_kernel(
    place_ref,
    lane0,
    lane1,
    lane2,
    lane3,
    feat0,
    feat1,
    feat2,
    feat3,
    w_source,
    w_target,
    w_radial,
    w_middle_t,
    w_output_t,
    w_onsite_a,
    w_onsite_b,
    out_ref,
    pairs,
    envelopes,
    source,
    target,
    onsite,
    mixer,
):
    domain = pl.program_id(0)
    quarter = pl.program_id(1)
    atoms = feat0.shape[0]
    half_atoms = atoms // 2
    tiles = half_atoms // pl.num_programs(1)
    domains = 4
    basis = w_radial.shape[0]

    @pl.when((domain == 0) & (quarter == 0))
    def prepare():
        place = place_ref[0]
        lanes = (lane0, lane1, lane2, lane3)
        feats = (feat0, feat1, feat2, feat3)
        for step in range(domains):
            where = place ^ step
            pairs[where] = lanes[step][...]
            reach = lanes[step][0]
            envelopes[where] = 0.5 * (jnp.cos(jnp.pi * reach / RADIUS) + 1.0)
            rows = feats[step][...]
            source[where] = dot(rows, w_source[...], NN)
            target[where] = dot(rows, w_target[...], NN)
            first = dot(rows, w_onsite_a[...], NN)
            second = dot(rows, w_onsite_b[...], NN)
            onsite[pl.ds(where * atoms, atoms), :] = 0.5 * (first + second)
        turned = onsite[...].astype(BF16).astype(F32)
        for column in range(onsite.shape[1] // LANES):
            piece = slice(column * LANES, (column + 1) * LANES)
            onsite[:, piece] = 0.5 * jnp.transpose(turned[:, piece])

    @pl.when(quarter == 0)
    def mix():
        following = lax.rem(domain + 1, domains)
        mixer[0:basis] = w_radial[...].astype(F32)
        mixer[basis : basis + atoms] = target[domain]
        mixer[basis + atoms : basis + 2 * atoms] = target[following]
        mixer[basis + 2 * atoms : basis + 3 * atoms] = source[domain]
        mixer[basis + 3 * atoms :] = jnp.zeros((mixer.shape[0] - basis - 3 * atoms, mixer.shape[1]), F32)
        mixer[...] = jnp.transpose(mixer[...])

    first_tile = quarter * tiles
    lane = lax.broadcasted_iota(jnp.int32, (1, LANES), 1)
    upper = lane >= LANES // 2
    sub128 = lax.broadcasted_iota(jnp.int32, (basis, LANES), 0)
    centres = RADIUS * sub128.astype(F32) / basis
    scale = 1.0 / (2.0 * RADIUS / basis)
    inputs = []
    envs = []
    names = []
    for u in range(tiles):
        reach = pairs[domain, 0, pl.ds(first_tile + u, 1), :]
        name = pairs[domain, 1, pl.ds(first_tile + u, 1), :].astype(jnp.int32)
        envs.append(envelopes[domain, pl.ds(first_tile + u, 1), :])
        names.append(name)
        radial_t = jnp.exp(-jnp.square((reach - centres) * scale))
        local = lax.rem(name - domain * atoms + domains * atoms, domains * atoms)
        who = first_tile + u + jnp.where(upper, half_atoms, 0)
        near = sub128[: 2 * atoms] == local
        mine = sub128[: 2 * atoms] == who
        inputs.append(
            jnp.concatenate(
                [radial_t, jnp.where(near, 1.0, 0.0), jnp.where(mine, 1.0, 0.0)], axis=0
            ).astype(BF16)
        )
    columns = jnp.concatenate(inputs, axis=1)
    hidden = silu(dot(mixer[...].astype(BF16), columns, NN)).astype(BF16)
    second = silu(dot(w_middle_t[...], hidden, NN)).astype(BF16)
    blocks = dot(w_output_t[...], second, NN)
    row2 = lax.broadcasted_iota(jnp.int32, (LANES, LANES), 0)
    column2 = lax.broadcasted_iota(jnp.int32, (LANES, LANES), 1)
    flags = jnp.concatenate(
        [jnp.where(column2 < LANES // 2, row2, -2), jnp.where(column2 < LANES // 2, -2, row2)], axis=0
    )
    for u in range(tiles):
        piece = (blocks[:, u * LANES : (u + 1) * LANES] * envs[u]).astype(BF16)
        chosen = jnp.where(flags == names[u], 1.0, 0.0).astype(BF16)
        placed = dot(piece, chosen, NT)
        for h in range(2):
            atom = domain * atoms + h * half_atoms + first_tile + u
            whole = placed[:, h * LANES : (h + 1) * LANES]
            for j in range(ORB):
                part = whole[j * PAD : (j + 1) * PAD]
                own = onsite_part(onsite, j)
                part = part + jnp.where(lane == atom, own, 0.0)
                out_ref[0, h, u * PAD : (u + 1) * PAD, j * LANES : (j + 1) * LANES] = part.astype(BF16)


def onsite_part(onsite, j):
    rows = j * PAD
    column = rows // LANES
    start = rows - column * LANES
    return onsite[start : start + PAD, column * LANES : (column + 1) * LANES]


def run_network(place, lanes, feats, weights):
    atoms = feats[0].shape[0]
    domains = len(feats)
    quarters = 4
    half_atoms = atoms // 2
    width = ORB * LANES
    rows = half_atoms // quarters * PAD
    hidden = weights[0].shape[1]
    vmem = pl.BlockSpec(memory_space=pltpu.VMEM)
    return pl.pallas_call(
        network_kernel,
        grid=(domains, quarters),
        out_shape=jax.ShapeDtypeStruct((domains, 2, half_atoms * PAD, width), BF16),
        in_specs=[pl.BlockSpec(memory_space=pltpu.SMEM)] + [vmem] * (2 * domains + len(weights)),
        out_specs=pl.BlockSpec((1, 2, rows, width), lambda d, q: (d, 0, q, 0)),
        scratch_shapes=[
            pltpu.VMEM((domains,) + lanes[0].shape, F32),
            pltpu.VMEM((domains,) + lanes[0].shape[1:], F32),
            pltpu.VMEM((domains, atoms, hidden), F32),
            pltpu.VMEM((domains, atoms, hidden), F32),
            pltpu.VMEM((domains * atoms, 2 * LANES), F32),
            pltpu.VMEM((hidden, hidden), F32),
        ],
        compiler_params=pltpu.CompilerParams(vmem_limit_bytes=VMEM_LIMIT),
        name="pair_network",
    )(place, *lanes, *feats, *weights)


def factor_panels(gram):
    order = gram.shape[0]
    count = order // PANEL
    row = lax.broadcasted_iota(jnp.int32, (PANEL, order), 0)
    lane = lax.broadcasted_iota(jnp.int32, (PANEL, order), 1)
    work = [gram[q * PANEL : (q + 1) * PANEL] for q in range(count)]
    extra = [jnp.where(lane == row + q * PANEL, 1.0, 0.0) for q in range(count)]
    upper = []
    inverse = []
    for p in range(count):
        base = p * PANEL
        block = [jnp.broadcast_to(work[p][:, base + k : base + k + 1], (PANEL, order)) for k in range(PANEL)]
        unit = [jnp.where(row == c, 1.0, 0.0) for c in range(PANEL)]
        for r in range(PANEL):
            pivot = spread_rows(block[r], r, PANEL)
            root = lax.rsqrt(pivot)
            column = jnp.where(row > r, block[r] * root, 0.0)
            for k in range(r + 1, PANEL):
                block[k] = block[k] - column * spread_rows(column, k, PANEL)
            for c in range(r + 1):
                lead = spread_rows(unit[c], r, PANEL) * root
                unit[c] = jnp.where(row == r, lead, unit[c] - column * lead)
        top = unit[0] * spread_rows(work[p], 0, PANEL)
        side = unit[0] * spread_rows(extra[p], 0, PANEL)
        for c in range(1, PANEL):
            top = top + unit[c] * spread_rows(work[p], c, PANEL)
            side = side + unit[c] * spread_rows(extra[p], c, PANEL)
        top = jnp.where(lane >= row + base, top, 0.0)
        upper.append(top)
        inverse.append(side)
        if p + 1 < count:
            high = top.astype(BF16)
            left = top - high.astype(F32)
            middle = left.astype(BF16)
            low = (left - middle.astype(F32)).astype(BF16)
            both = jnp.concatenate([top, side], axis=1)
            bhigh = both.astype(BF16)
            bleft = both - bhigh.astype(F32)
            bmiddle = bleft.astype(BF16)
            blow = (bleft - bmiddle.astype(F32)).astype(BF16)
            lhs = jnp.concatenate([high, high, middle, middle, high, low], axis=0)
            rhs = jnp.concatenate([bhigh, bmiddle, bhigh, bmiddle, blow, bhigh], axis=0)
            change = dot(lhs, rhs, TN)
            for q in range(p + 1, count):
                rows = slice(q * PANEL, (q + 1) * PANEL)
                work[q] = work[q] - change[rows, :order]
                extra[q] = extra[q] - change[rows, order:]
    return jnp.concatenate(upper, axis=0), jnp.concatenate(inverse, axis=0)


def lanczos_kernel(
    place_ref,
    x_own,
    x_left1,
    x_left2,
    x_left3,
    x_right1,
    x_right2,
    x_right3,
    pairs_hbm,
    alpha_ref,
    beta_ref,
    next_ref,
    pairs,
    xs,
    ys,
    qs,
    flat,
    turned,
    sem,
    rows_total,
):
    copy = pltpu.make_async_copy(pairs_hbm, pairs, sem)
    copy.start()
    place = place_ref[0]
    atoms = x_own.shape[0]
    half = atoms // 2
    states = x_own.shape[2]
    total = xs.shape[0]
    atoms_all = total // PAD
    chunk = 512
    chunks = total // chunk
    scale = 1.0 / rows_total

    zero = jnp.zeros((PAD - ORB, states), F32)

    def take(source, base):
        for atom in range(source.shape[0]):
            start = pl.multiple_of((base + atom) * PAD, PAD)
            xs[pl.ds(start, ORB), :] = source[atom]
            xs[pl.ds(start + ORB, PAD - ORB), :] = zero

    take(x_own, place * atoms)
    low = place_ref[1]
    for step, (mine, other) in enumerate(
        ((x_left1, x_right1), (x_left2, x_right2), (x_left3, x_right3)), 1
    ):
        base = (place ^ step) * atoms
        take(mine, base + low * half)
        take(other, base + (1 - low) * half)

    def rows_of(ref, index):
        return ref[pl.ds(pl.multiple_of(index * chunk, chunk), chunk), :]

    def put(ref, index, value):
        ref[pl.ds(pl.multiple_of(index * chunk, chunk), chunk), :] = value

    def own_gram(pieces):
        high, low_part = pieces
        cross = dot(high, low_part, TN)
        return dot(high, high, TN) + cross + jnp.transpose(cross)

    def apply(ref):
        for j in range(ORB):
            flat_rows = slice(j * LANES, (j + 1) * LANES)
            high, low_part = split(ref[pl.ds(j, atoms_all, stride=PAD), :])
            flat[flat_rows, :states] = high
            flat[flat_rows, states:] = low_part
        for index in range(chunks):
            high, low_part = split(rows_of(ref, index))
            turned[:states, index * chunk : (index + 1) * chunk] = jnp.transpose(high)
            turned[states:, index * chunk : (index + 1) * chunk] = jnp.transpose(low_part)

        def forward(index, carry):
            both = dot(rows_of(pairs, index), flat[...], NN)
            put(ys, index, both[:, :states] + both[:, states:])
            return carry

        lax.fori_loop(0, chunks, forward, 0)
        for j in range(ORB):
            both = dot(turned[...], pairs[:, j * LANES : (j + 1) * LANES], NN)
            back = jnp.transpose(both[:states] + both[states:])
            ys[pl.ds(j, atoms_all, stride=PAD), :] = ys[pl.ds(j, atoms_all, stride=PAD), :] + back

    def loop(function, results):
        return lax.fori_loop(0, chunks, function, tuple(jnp.zeros((states, states), F32) for _ in range(results)))

    def gram_start(index, carry):
        return (carry[0] + own_gram(split(rows_of(xs, index))),)

    (gram,) = loop(gram_start, 1)
    factor, inverse = factor_panels(gram * scale)
    copy.wait()
    apply(xs)
    inverse = split(inverse)

    def first_alpha(index, carry):
        current = dot_split(split(rows_of(xs, index)), inverse, NT)
        residue = dot_split(split(rows_of(ys, index)), inverse, NT)
        put(qs, index, current)
        put(ys, index, residue)
        return (carry[0] + dot_split(split(current), split(residue), TN),)

    (alpha,) = loop(first_alpha, 1)
    alpha = alpha * scale
    alpha_ref[0] = alpha
    alpha = split(alpha)

    def first_gram(index, carry):
        residue = rows_of(ys, index) - dot_split(split(rows_of(qs, index)), alpha, NN)
        put(xs, index, residue)
        return (carry[0] + own_gram(split(residue)),)

    (gram,) = loop(first_gram, 1)
    factor, inverse = factor_panels(gram * scale)
    beta_ref[0] = factor
    apply(xs)
    inverse = split(inverse)
    factor = split(factor)

    def second_alpha(index, carry):
        current = dot_split(split(rows_of(xs, index)), inverse, NT)
        residue = dot_split(split(rows_of(ys, index)), inverse, NT)
        residue = residue - dot_split(split(rows_of(qs, index)), factor, NT)
        put(xs, index, current)
        put(ys, index, residue)
        return (carry[0] + dot_split(split(current), split(residue), TN),)

    (alpha,) = loop(second_alpha, 1)
    alpha = alpha * scale
    alpha_ref[1] = alpha
    alpha = split(alpha)

    def second_gram(index, carry):
        residue = rows_of(ys, index) - dot_split(split(rows_of(xs, index)), alpha, NN)
        put(ys, index, residue)
        return (carry[0] + own_gram(split(residue)),)

    (gram,) = loop(second_gram, 1)
    factor, inverse = factor_panels(gram * scale)
    beta_ref[1] = factor
    inverse = split(inverse)
    mine = dot_split(split(rows_of(ys, place)), inverse, NT)
    next_ref[...] = mine.reshape(atoms, PAD, states)[:, :ORB, :]


def run_lanczos(place, own, left, right, pairs, rows_total):
    atoms, _, states = own.shape
    total = pairs.shape[0]
    vmem = pl.BlockSpec(memory_space=pltpu.VMEM)

    def kernel(*refs):
        lanczos_kernel(*refs, rows_total)

    return pl.pallas_call(
        kernel,
        out_shape=(
            jax.ShapeDtypeStruct((STEPS, states, states), F32),
            jax.ShapeDtypeStruct((STEPS, states, states), F32),
            jax.ShapeDtypeStruct(own.shape, F32),
        ),
        in_specs=[pl.BlockSpec(memory_space=pltpu.SMEM)] + [vmem] * 7 + [pl.BlockSpec(memory_space=pl.ANY)],
        out_specs=(vmem, vmem, vmem),
        scratch_shapes=[
            pltpu.VMEM(pairs.shape, BF16),
            pltpu.VMEM((total, states), F32),
            pltpu.VMEM((total, states), F32),
            pltpu.VMEM((total, states), F32),
            pltpu.VMEM((pairs.shape[1], 2 * states), BF16),
            pltpu.VMEM((2 * states, total), BF16),
            pltpu.SemaphoreType.DMA,
        ],
        compiler_params=pltpu.CompilerParams(vmem_limit_bytes=VMEM_LIMIT),
        name="block_lanczos",
    )(place, own, *left, *right, pairs)


def exchange(shard, axis, mask):
    devices = lax.axis_size(axis)
    return lax.ppermute(shard, axis, [(i, i ^ mask) for i in range(devices)])


def body(
    node_feats,
    distance,
    neighbours,
    counts,
    w_source,
    w_target,
    w_radial,
    w_middle,
    w_output,
    w_onsite,
    initial,
):
    atoms_here, slots_here = neighbours.shape
    domains = lax.axis_size("dom")
    members = lax.axis_size("st") * lax.axis_size("sub")
    atoms_all = atoms_here * domains
    suits = (domains, atoms_all, 2 * members * slots_here, initial.shape[2]) == (4, LANES, LANES, LANES)
    if not (suits and lax.axis_size("sub") == 2 and lax.axis_size("st") == 2):
        return body_spread(
            node_feats,
            distance,
            neighbours,
            counts,
            w_source,
            w_target,
            w_radial,
            w_middle,
            w_output,
            w_onsite,
            initial,
        )
    domain = lax.axis_index("dom")
    core = lax.axis_index("sub")
    member = lax.axis_index(("st", "sub"))
    place = jnp.stack([domain, core]).astype(jnp.int32)

    slot_index = member * slots_here + jnp.arange(slots_here, dtype=jnp.int32)
    usable = slot_index[None, :] < counts[:, None]
    named = jnp.where(usable, neighbours, -1).astype(F32)
    own = jnp.stack([distance, named]).reshape(2, 2, atoms_here // 2, 1, slots_here)
    own = jnp.where((jnp.arange(members) == member)[:, None], own, 0.0)
    own = jnp.swapaxes(own, 1, 2).reshape(2, atoms_here // 2, LANES)
    own = own + exchange(own, "sub", 1)
    own = own + exchange(own, "st", 1)

    lanes = [own] + [exchange(own, "dom", step) for step in range(1, domains)]
    feats = [node_feats] + [exchange(node_feats, "dom", step) for step in range(1, domains)]
    half = atoms_here // 2
    part = lax.dynamic_slice_in_dim(initial, core * half, half, 0)
    left = [exchange(part, "dom", step) for step in range(1, domains)]
    right = [exchange(piece, "sub", 1) for piece in left]

    def blocks_of(weights, order):
        blocks = weights.reshape(-1, ORB, ORB).transpose(order)
        return blocks

    columns = jnp.pad(blocks_of(w_output, (2, 1, 0)), ((0, 0), (0, PAD - ORB), (0, 0)))
    w_output_t = columns.reshape(ORB * PAD, -1)
    spare = 2 * LANES - ORB * PAD

    def onsite_weights(order):
        blocks = jnp.pad(blocks_of(w_onsite, order), ((0, 0), (0, 0), (0, PAD - ORB)))
        return jnp.pad(blocks.reshape(-1, ORB * PAD), ((0, 0), (0, spare)))

    weights = (
        w_source,
        w_target,
        w_radial,
        w_middle.T,
        w_output_t,
        onsite_weights((0, 2, 1)),
        onsite_weights((0, 1, 2)),
    )
    pairs = run_network(place, lanes, feats, weights)
    pairs = pairs.reshape(atoms_all * PAD, ORB * LANES)
    return run_lanczos(place, initial, left, right, pairs, float(atoms_all * ORB))


def solution(mesh):
    placed = (
        P(("grp", "dom"), None),
        P(("grp", "dom"), ("st", "sub")),
        P(("grp", "dom"), ("st", "sub")),
        P(("grp", "dom")),
        P(),
        P(),
        P(),
        P(),
        P(),
        P(),
        P(("grp", "dom"), None, None),
    )
    return jax.shard_map(
        body,
        mesh=mesh,
        in_specs=placed,
        out_specs=(P("grp", None, None), P("grp", None, None), P(("grp", "dom"), None, None)),
        check_vma=False,
    )
```

```python
import jax
import jax.numpy as jnp
from jax import lax
from jax.experimental import pallas as pl
from jax.experimental.pallas import tpu as pltpu
from jax.sharding import PartitionSpec as P

ORB = 13
STEPS = 2


RADIUS = 7.0


def shifted(shard, axis, by):
    devices = lax.axis_size(axis)
    return lax.ppermute(shard, axis, [(i, (i + by) % devices) for i in range(devices)])


def radial(distance, basis_count):
    centres = RADIUS * jnp.arange(basis_count, dtype=jnp.float32) / basis_count
    spacing = RADIUS / basis_count
    return jnp.exp(-jnp.square((distance[..., None] - centres) / (2.0 * spacing)))


def envelope(distance, usable):
    return 0.5 * (jnp.cos(jnp.pi * distance / RADIUS) + 1.0) * usable.astype(jnp.float32)


def onsite_blocks(node_feats, w_onsite):
    projected = jnp.dot(node_feats, w_onsite, preferred_element_type=jnp.float32)
    matrix = projected.reshape(-1, ORB, ORB)
    return (0.5 * (matrix + jnp.swapaxes(matrix, 1, 2))).astype(jnp.bfloat16)


def pair_blocks(source_rows, target_rows, distance, usable, w_radial, w_middle, w_output):
    radial_basis = radial(distance, w_radial.shape[0]).astype(jnp.bfloat16)
    mixed = source_rows[:, None, :].astype(jnp.float32) + target_rows.astype(jnp.float32)
    mixed = mixed + jnp.dot(radial_basis, w_radial, preferred_element_type=jnp.float32)
    hidden_one = jax.nn.silu(mixed).astype(jnp.bfloat16)
    second = jax.nn.silu(jnp.dot(hidden_one, w_middle, preferred_element_type=jnp.float32)).astype(
        jnp.bfloat16
    )
    output_blocks = (
        jnp.dot(second, w_output, preferred_element_type=jnp.float32)
        * envelope(distance, usable)[..., None]
    )
    return output_blocks.astype(jnp.bfloat16).reshape(
        distance.shape[0], distance.shape[1], ORB, ORB
    )


def gram_matrix(left, right, rows_total):
    return jnp.einsum("ris,rit->st", left, right, precision=lax.Precision.HIGHEST) / rows_total


def combine(states, matrix):
    return jnp.einsum("ris,st->rit", states, matrix, precision=lax.Precision.HIGHEST)


def upper_factor(matrix):
    order = matrix.shape[0]
    places = jnp.arange(order, dtype=jnp.int32)

    def column_step(column_index, carry):
        work, lower = carry
        column = lax.dynamic_slice_in_dim(work, column_index, 1, 1)[:, 0]
        pivot = jnp.sqrt(lax.dynamic_slice_in_dim(column, column_index, 1, 0)[0])
        scaled = jnp.where(places >= column_index, column / pivot, jnp.zeros_like(column))
        work = work - scaled[:, None] * scaled[None, :]
        lower = lax.dynamic_update_slice_in_dim(lower, scaled[:, None], column_index, 1)
        return (work, lower)

    work, lower = lax.fori_loop(0, order, column_step, (matrix, jnp.zeros_like(matrix)))
    return lower.T


def upper_inverse(factor):
    order = factor.shape[0]
    identity = jnp.eye(order, dtype=factor.dtype)

    def row_step(counter, inverse):
        row_index = order - 1 - counter
        factor_row = lax.dynamic_slice_in_dim(factor, row_index, 1, 0)
        unit_row = lax.dynamic_slice_in_dim(identity, row_index, 1, 0)
        pivot = lax.dynamic_slice_in_dim(factor_row[0], row_index, 1, 0)[0]
        known = jnp.dot(factor_row, inverse, precision=lax.Precision.HIGHEST)
        fresh = (unit_row - known) / pivot
        return lax.dynamic_update_slice_in_dim(inverse, fresh, row_index, 0)

    return lax.fori_loop(0, order, row_step, jnp.zeros_like(factor))


def divide_right(residue, factor):
    return combine(residue, upper_inverse(factor))


def onsite_apply(onsite, states):
    return jnp.einsum("aij,ajs->ais", onsite, states, precision=lax.Precision.HIGHEST)


def lanczos(states, operate, totals, rows_total):
    factor = upper_factor(totals(gram_matrix(states, states, rows_total)))
    current = divide_right(states, factor)
    previous = current
    beta_prev = factor
    alpha_list = []
    beta_list = []
    for iteration in range(STEPS):
        residue = operate(current)
        if iteration > 0:
            residue = residue - combine(previous, beta_prev.T)
        alpha_block = totals(gram_matrix(current, residue, rows_total))
        residue = residue - combine(current, alpha_block)
        beta_block = upper_factor(totals(gram_matrix(residue, residue, rows_total)))
        previous = current
        current = divide_right(residue, beta_block)
        beta_prev = beta_block
        alpha_list.append(alpha_block)
        beta_list.append(beta_block)
    return (jnp.stack(alpha_list), jnp.stack(beta_list), current)


def body_spread(
    node_feats,
    distance,
    neighbours,
    counts,
    w_source,
    w_target,
    w_radial,
    w_middle,
    w_output,
    w_onsite,
    initial,
):
    atoms_here = node_feats.shape[0]
    slots_here = neighbours.shape[1]
    domain = lax.axis_index("dom")
    member = lax.axis_index(("st", "sub"))
    atoms_all = atoms_here * lax.axis_size("dom")
    rows_total = float(atoms_all * ORB)
    ghost_feats = shifted(node_feats, "dom", -1)
    local_index = (neighbours - domain * atoms_here) % atoms_all
    source = jnp.dot(node_feats, w_source, preferred_element_type=jnp.float32).astype(jnp.bfloat16)
    combined_feats = jnp.concatenate([node_feats, ghost_feats], axis=0)
    target = jnp.dot(combined_feats, w_target, preferred_element_type=jnp.float32).astype(
        jnp.bfloat16
    )
    slot_index = member * slots_here + jnp.arange(slots_here, dtype=jnp.int32)
    usable = slot_index[None, :] < counts[:, None]
    blocks = pair_blocks(
        source, target[local_index], distance, usable, w_radial, w_middle, w_output
    ).astype(jnp.float32)

    def edge_terms(whole_rows, ghost_rows):
        combined = jnp.concatenate([whole_rows, ghost_rows], axis=0)
        forward = jnp.einsum(
            "akij,akjs->ais", blocks, combined[local_index], precision=lax.Precision.HIGHEST
        )
        backward = jnp.einsum("akij,ais->akjs", blocks, whole_rows, precision=lax.Precision.HIGHEST)
        spread = jax.ops.segment_sum(
            backward.reshape(-1, ORB, whole_rows.shape[-1]),
            local_index.reshape(-1),
            num_segments=2 * atoms_here,
        )
        arrived = shifted(spread[atoms_here:], "dom", 1)
        return forward + spread[:atoms_here] + arrived

    onsite = onsite_blocks(node_feats, w_onsite).astype(jnp.float32)

    def operate(current):
        ghost_rows = shifted(current, "dom", -1)
        summed = lax.psum(edge_terms(current, ghost_rows), ("st", "sub"))
        return summed + onsite_apply(onsite, current)

    def totals(value):
        return lax.psum(value, "dom")

    alpha_blocks, beta_blocks, final_rows = lanczos(initial, operate, totals, rows_total)
    return (alpha_blocks, beta_blocks, final_rows)


F32 = jnp.float32
BF16 = jnp.bfloat16
LANES = 128
PAD = 16
PANEL = 8
NEAR = 3
VMEM_LIMIT = 56 * 1024 * 1024


def dims(left, right):
    return (((left,), (right,)), ((), ()))


def dot(left, right, contract):
    return lax.dot_general(left, right, contract, preferred_element_type=F32)


def split(value):
    high = value.astype(BF16)
    return high, (value - high.astype(F32)).astype(BF16)


def dot_split(left, right, contract):
    lh, ll = left
    rh, rl = right
    return dot(lh, rh, contract) + (dot(ll, rh, contract) + dot(lh, rl, contract))


NN = dims(1, 0)
NT = dims(1, 1)
TN = dims(0, 0)


def silu(value):
    half = 0.5 * value
    return half + half * jnp.tanh(half)


def spread_rows(value, row, count):
    return jnp.broadcast_to(value[row : row + 1, :], (count, value.shape[1]))


def lanes_kernel(place_ref, distance, named, counts, out_ref):
    slots, atoms = distance.shape
    member = place_ref[2]
    slot = lax.broadcasted_iota(jnp.int32, (slots, atoms), 0) + member * slots
    usable = slot < counts[...]
    names = jnp.where(usable, named[...], -1).astype(F32)
    turned = jnp.transpose(jnp.concatenate([distance[...], names], axis=0))
    group = atoms // 4
    space = jnp.zeros((2 * group, LANES // 2 - slots), F32)
    for kind in range(2):
        part = turned[:, kind * slots : (kind + 1) * slots]
        first = jnp.concatenate([part[:group], part[2 * group : 3 * group]], axis=0)
        second = jnp.concatenate([part[group : 2 * group], part[3 * group :]], axis=0)
        row = jnp.concatenate([first, space, second, space], axis=1)
        out_ref[kind] = pltpu.roll(row, member * slots, 1)


def run_lanes(place, distance, named, counts):
    vmem = pl.BlockSpec(memory_space=pltpu.VMEM)
    return pl.pallas_call(
        lanes_kernel,
        out_shape=jax.ShapeDtypeStruct((2, distance.shape[1] // 2, LANES), F32),
        in_specs=[pl.BlockSpec(memory_space=pltpu.SMEM), vmem, vmem, vmem],
        out_specs=vmem,
        name="slot_lanes",
    )(place, distance, named, counts)


def network_kernel(
    place_ref,
    pack0,
    pack1,
    pack2,
    pack3,
    w_source,
    w_target,
    w_radial,
    w_middle,
    w_output_t,
    w_onsite_t,
    out_ref,
    pairs,
    envelopes,
    source,
    target,
    onsite,
    feats,
    mixer,
    middle,
    outer,
    raw,
    rows,
    placed_ref,
):
    domain = pl.program_id(0)
    group = pl.program_id(1)
    domains = 4
    groups = pl.num_programs(1)
    atoms = source.shape[1]
    tiles = atoms // 4
    basis = w_radial.shape[0]
    stride = ORB * PAD

    @pl.when((domain == 0) & (group == 0))
    def prepare():
        place = place_ref[0]
        for step, pack in enumerate((pack0, pack1, pack2, pack3)):
            where = place ^ step
            reach = pack[: 2 * tiles]
            pairs[where, 0] = reach
            pairs[where, 1] = pack[2 * tiles : 4 * tiles]
            envelopes[where] = 0.5 * (jnp.cos(jnp.pi * reach / RADIUS) + 1.0)
            got = jnp.concatenate([pack[4 * tiles : 4 * tiles + atoms], pack[4 * tiles + atoms :]], axis=1)
            got = got.astype(BF16)
            source[where] = dot(got, w_source[...], NN)
            target[where] = dot(got, w_target[...], NN)
            feats[where] = got
        middle[...] = jnp.transpose(w_middle[...].astype(F32)).astype(BF16)
        empty = jnp.zeros((PAD - ORB, rows.shape[1]), F32)

        def fill_raw(weights):
            for side in range(raw.shape[0]):
                raw[side] = weights[:, side * LANES : (side + 1) * LANES].astype(F32)

        def read_raw(where):
            return jnp.concatenate([raw[side, where, :] for side in range(raw.shape[0])], axis=1)

        def arrange(read):
            for j in range(ORB):
                rows[j * PAD : j * PAD + ORB, :] = read(j)
                rows[j * PAD + ORB : (j + 1) * PAD, :] = empty
            return rows[...].astype(BF16)

        whole = feats[...].reshape(domains * atoms, feats.shape[2])
        fill_raw(w_onsite_t)
        first = dot(arrange(lambda j: read_raw(pl.ds(j, ORB, stride=ORB))), whole, NT)
        second = dot(arrange(lambda j: read_raw(pl.ds(j * ORB, ORB))), whole, NT)
        onsite[...] = 0.5 * (0.5 * (first + second)).astype(BF16).astype(F32)
        fill_raw(w_output_t)
        outer[...] = arrange(lambda j: read_raw(pl.ds(j, ORB, stride=ORB)))

    @pl.when(group == 0)
    def mix():
        following = lax.rem(domain + 1, domains)
        spare = mixer.shape[1] - basis - 3 * atoms
        stacked = jnp.concatenate(
            [
                w_radial[...].astype(F32),
                target[domain],
                target[following],
                source[domain],
                jnp.zeros((spare, mixer.shape[0]), F32),
            ],
            axis=0,
        )
        mixer[...] = jnp.transpose(stacked).astype(BF16)

    lane = lax.broadcasted_iota(jnp.int32, (1, LANES), 1)
    upper = lane >= LANES // 2
    row2 = lax.broadcasted_iota(jnp.int32, (LANES, LANES), 0)
    column2 = lax.broadcasted_iota(jnp.int32, (LANES, LANES), 1)
    centres = RADIUS * row2.astype(F32) / basis
    scale = 1.0 / (2.0 * RADIUS / basis)
    inputs = []
    envs = []
    names = []
    for u in range(tiles):
        line = pl.ds(group * tiles + u, 1)
        reach = pairs[domain, 0, line, :]
        name = pairs[domain, 1, line, :].astype(jnp.int32)
        envs.append(envelopes[domain, line, :])
        names.append(name)
        radial_t = jnp.exp(-jnp.square((reach - centres) * scale))
        local = lax.rem(name - domain * atoms + domains * atoms, domains * atoms)
        who = group * 2 * tiles + u + jnp.where(upper, tiles, 0)
        near = row2[: 2 * atoms] == local
        mine = row2[: 2 * atoms] == who
        inputs.append(
            jnp.concatenate(
                [radial_t, jnp.where(near, 1.0, 0.0), jnp.where(mine, 1.0, 0.0)], axis=0
            ).astype(BF16)
        )
    columns = jnp.concatenate(inputs, axis=1)
    hidden = silu(dot(mixer[...], columns, NN)).astype(BF16)
    second = silu(dot(middle[...], hidden, NN)).astype(BF16)
    blocks = dot(outer[...], second, NN)
    flags = jnp.concatenate(
        [jnp.where(column2 < LANES // 2, row2, -2), jnp.where(column2 < LANES // 2, -2, row2)], axis=0
    )
    for u in range(tiles):
        piece = (blocks[:, u * LANES : (u + 1) * LANES] * envs[u]).astype(BF16)
        chosen = jnp.where(flags == names[u], 1.0, 0.0).astype(BF16)
        placed = dot(piece, chosen, NT)
        for h in range(2):
            place = h * tiles + u
            atom = domain * atoms + group * 2 * tiles + place
            whole = placed[:, h * LANES : (h + 1) * LANES] + jnp.where(lane == atom, onsite[...], 0.0)
            rows_at = slice(place * stride, (place + 1) * stride)
            placed_ref[rows_at, :] = whole
    for j in range(ORB):
        for i in range(ORB):
            tile = placed_ref[pl.ds(j * PAD + i, 2 * tiles, stride=stride), :]
            out_ref[i, :, j * LANES : (j + 1) * LANES] = tile.astype(BF16)


def run_network(place, packs, weights):
    domains = len(packs)
    atoms = packs[0].shape[0] // 3
    groups = 2
    width = ORB * LANES
    tiles = atoms // 4
    hidden = weights[0].shape[1]
    vmem = pl.BlockSpec(memory_space=pltpu.VMEM)
    return pl.pallas_call(
        network_kernel,
        grid=(domains, groups),
        out_shape=jax.ShapeDtypeStruct((ORB, domains * atoms, width), BF16),
        in_specs=[pl.BlockSpec(memory_space=pltpu.SMEM)] + [vmem] * (domains + len(weights)),
        out_specs=pl.BlockSpec((ORB, 2 * tiles, width), lambda d, g: (0, groups * d + g, 0)),
        scratch_shapes=[
            pltpu.VMEM((domains, 2, 2 * tiles, LANES), F32),
            pltpu.VMEM((domains, 2 * tiles, LANES), F32),
            pltpu.VMEM((domains, atoms, hidden), F32),
            pltpu.VMEM((domains, atoms, hidden), F32),
            pltpu.VMEM((ORB * PAD, LANES), F32),
            pltpu.VMEM((domains, atoms, weights[0].shape[0]), BF16),
            pltpu.VMEM((hidden, hidden), BF16),
            pltpu.VMEM((hidden, hidden), BF16),
            pltpu.VMEM((ORB * PAD, hidden), BF16),
            pltpu.VMEM((hidden // LANES, ORB * ORB, LANES), F32),
            pltpu.VMEM((ORB * PAD, hidden), F32),
            pltpu.VMEM((2 * tiles * ORB * PAD, LANES), F32),
        ],
        compiler_params=pltpu.CompilerParams(vmem_limit_bytes=VMEM_LIMIT),
        cost_estimate=pl.CostEstimate(flops=6_000_000_000, bytes_accessed=8_000_000, transcendentals=6_000_000),
        name="pair_network",
    )(place, *packs, *weights)


def column_of(value, lane):
    return jnp.broadcast_to(value[:, lane : lane + 1], (value.shape[0], LANES))


def split_three(value):
    high = value.astype(BF16)
    rest = value - high.astype(F32)
    middle = rest.astype(BF16)
    return high, middle, (rest - middle.astype(F32)).astype(BF16)


def outer_change(top, side):
    high, middle, low = split_three(top)
    sides = split_three(side)
    wide = [jnp.concatenate([t, s], axis=1) for t, s in zip((high, middle, low), sides)]
    left = jnp.concatenate([high, high, middle, middle, high, low], axis=0)
    right = jnp.concatenate([wide[0], wide[1], wide[0], wide[1], wide[2], wide[0]], axis=0)
    return dot(left, right, TN)


def factor_panels(gram, fill=()):
    order = gram.shape[0]
    count = order // PANEL
    row = lax.broadcasted_iota(jnp.int32, (PANEL, order), 0)
    lane = lax.broadcasted_iota(jnp.int32, (PANEL, order), 1)
    work = [gram[q * PANEL : (q + 1) * PANEL] for q in range(count)]
    extra = [jnp.where(lane == row + q * PANEL, 1.0, 0.0) for q in range(count)]
    upper = []
    inverse = []
    block = [column_of(work[0], k) for k in range(PANEL)]
    for p in range(count):
        base = p * PANEL
        near = [q for q in range(p + 1, min(p + 1 + NEAR, count))]
        beside = {q: [column_of(work[q], base + c) for c in range(PANEL)] for q in near}
        following = [column_of(work[p + 1], base + PANEL + k) for k in range(PANEL)] if near else []
        unit = [jnp.where(row == c, 1.0, 0.0) for c in range(PANEL)]
        roots = jnp.zeros((PANEL, order), F32)
        for r in range(PANEL):
            root = lax.rsqrt(spread_rows(block[r], r, PANEL))
            column = jnp.where(row > r, block[r] * root, 0.0)
            rows = {k: spread_rows(column, k, PANEL) for k in range(r + 1, PANEL)}
            for k in range(r + 1, PANEL):
                block[k] = block[k] - column * rows[k]
            for q in near:
                beside[q][r] = beside[q][r] * root
                for k in range(r + 1, PANEL):
                    beside[q][k] = beside[q][k] - beside[q][r] * rows[k]
            ratio = column * root
            for c in range(r + 1):
                unit[c] = unit[c] - ratio * spread_rows(unit[c], r, PANEL)
            roots = jnp.where(row == r, root, roots)
            if near:
                done = beside[p + 1][r]
                for k in range(PANEL):
                    following[k] = following[k] - done * spread_rows(done, k, PANEL)
        if p < len(fill):
            fill[p]()
        top = unit[0] * spread_rows(work[p], 0, PANEL)
        side = unit[0] * spread_rows(extra[p], 0, PANEL)
        for c in range(1, PANEL):
            top = top + unit[c] * spread_rows(work[p], c, PANEL)
            side = side + unit[c] * spread_rows(extra[p], c, PANEL)
        top = jnp.where(lane >= row + base, top * roots, 0.0)
        side = side * roots
        upper.append(top)
        inverse.append(side)
        if near:
            tops = [spread_rows(top, c, PANEL) for c in range(PANEL)]
            sides = [spread_rows(side, c, PANEL) for c in range(PANEL)]
            for q in near:
                for c in range(PANEL):
                    work[q] = work[q] - beside[q][c] * tops[c]
                    extra[q] = extra[q] - beside[q][c] * sides[c]
            if p + 1 + NEAR < count:
                change = outer_change(top, side)
                for q in range(p + 1 + NEAR, count):
                    rows = slice(q * PANEL, (q + 1) * PANEL)
                    work[q] = work[q] - change[rows, :order]
                    extra[q] = extra[q] - change[rows, order:]
            block = following
    return jnp.concatenate(upper, axis=0), jnp.concatenate(inverse, axis=0)


def lanczos_kernel(
    place_ref,
    x_own,
    x_left1,
    x_left2,
    x_left3,
    x_right1,
    x_right2,
    x_right3,
    pairs_hbm,
    alpha_ref,
    beta_ref,
    next_ref,
    pairs,
    xs,
    ys,
    qs,
    flat,
    sem,
    rows_total,
):
    copy = pltpu.make_async_copy(pairs_hbm, pairs, sem)
    copy.start()
    place = place_ref[0]
    core = place_ref[1]
    orbitals, atoms, states = x_own.shape
    half = atoms // 2
    total = flat.shape[0]
    scale = 1.0 / rows_total

    def take(source, base):
        xs[:, pl.ds(pl.multiple_of(base, half), source.shape[1]), :] = source[...]

    take(x_own, place * atoms)
    for step, (mine, other) in enumerate(
        ((x_left1, x_right1), (x_left2, x_right2), (x_left3, x_right3)), 1
    ):
        base = (place ^ step) * atoms
        take(mine, base + core * half)
        take(other, base + (1 - core) * half)

    def whole(ref):
        return ref[...].reshape(total, states)

    def own_gram(pieces):
        high, low = pieces
        both = dot(high, jnp.concatenate([high, low], axis=1), TN)
        cross = both[:, states:]
        return (both[:, :states] + (cross + jnp.transpose(cross))) * scale

    def set_flat(pieces):
        flat[:, :states] = pieces[0]
        flat[:, states:] = pieces[1]

    chunk = 208
    width = 256

    def forward(start):
        def run():
            both = dot(pairs[start : start + chunk, :], flat[...], NN)
            ys[start : start + chunk, :] = both[:, :states] + both[:, states:]

        return run

    def backward(start):
        stop = min(start + width, total)

        def run():
            both = dot(pairs[:, start:stop], flat[...], TN)
            ys[start:stop, :] = ys[start:stop, :] + (both[:, :states] + both[:, states:])

        return run

    fill = [forward(start) for start in range(0, total, chunk)]
    fill = fill + [backward(start) for start in range(0, total, width)]

    pieces = split(whole(xs))
    set_flat(pieces)
    gram = own_gram(pieces)
    copy.wait()
    factor, inverse = factor_panels(gram, fill)
    inverse = split(inverse)
    current = dot_split(pieces, inverse, NT)
    first = split(current)
    qs[:, :states] = first[0]
    qs[:, states:] = first[1]
    residue = dot_split(split(ys[...]), inverse, NT)
    alpha = dot_split(first, split(residue), TN) * scale
    alpha_ref[0] = alpha
    residue = residue - dot_split(first, split(alpha), NN)
    pieces = split(residue)
    set_flat(pieces)
    gram = own_gram(pieces)
    factor, inverse = factor_panels(gram, fill)
    beta_ref[0] = factor
    inverse = split(inverse)
    current = dot_split((flat[:, :states], flat[:, states:]), inverse, NT)
    residue = dot_split(split(ys[...]), inverse, NT)
    residue = residue - dot_split((qs[:, :states], qs[:, states:]), split(factor), NT)
    first = split(current)
    alpha = dot_split(first, split(residue), TN) * scale
    alpha_ref[1] = alpha
    residue = residue - dot_split(first, split(alpha), NN)
    xs[...] = residue.reshape(xs.shape)
    gram = own_gram(split(residue))
    factor, inverse = factor_panels(gram)
    beta_ref[1] = factor
    mine = xs[:, pl.ds(pl.multiple_of(place * atoms, atoms), atoms), :].reshape(orbitals * atoms, states)
    mine = dot_split(split(mine), split(inverse), NT)
    next_ref[...] = mine.reshape(orbitals, atoms, states)


def run_lanczos(place, own, left, right, pairs, rows_total):
    states = own.shape[2]
    total = pairs.shape[0]
    vmem = pl.BlockSpec(memory_space=pltpu.VMEM)

    def kernel(*refs):
        lanczos_kernel(*refs, rows_total)

    return pl.pallas_call(
        kernel,
        out_shape=(
            jax.ShapeDtypeStruct((STEPS, states, states), F32),
            jax.ShapeDtypeStruct((STEPS, states, states), F32),
            jax.ShapeDtypeStruct(own.shape, F32),
        ),
        in_specs=[pl.BlockSpec(memory_space=pltpu.SMEM)] + [vmem] * 7 + [pl.BlockSpec(memory_space=pl.ANY)],
        out_specs=(vmem, vmem, vmem),
        scratch_shapes=[
            pltpu.VMEM(pairs.shape, BF16),
            pltpu.VMEM((own.shape[0], total // own.shape[0], states), F32),
            pltpu.VMEM((total, states), F32),
            pltpu.VMEM((total, 2 * states), BF16),
            pltpu.VMEM((total, 2 * states), BF16),
            pltpu.SemaphoreType.DMA,
        ],
        compiler_params=pltpu.CompilerParams(vmem_limit_bytes=VMEM_LIMIT),
        name="block_lanczos",
    )(place, own, *left, *right, pairs)


def exchange(shard, axis, mask):
    devices = lax.axis_size(axis)
    return lax.ppermute(shard, axis, [(i, i ^ mask) for i in range(devices)])


def body(
    node_feats,
    distance,
    neighbours,
    counts,
    w_source,
    w_target,
    w_radial,
    w_middle,
    w_output,
    w_onsite,
    initial,
):
    atoms_here, slots_here = neighbours.shape
    domains = lax.axis_size("dom")
    members = lax.axis_size("st") * lax.axis_size("sub")
    atoms_all = atoms_here * domains
    suits = (domains, atoms_all, 2 * members * slots_here, initial.shape[2]) == (4, LANES, LANES, LANES)
    if not (suits and lax.axis_size("sub") == 2 and lax.axis_size("st") == 2):
        return body_spread(
            node_feats,
            distance,
            neighbours,
            counts,
            w_source,
            w_target,
            w_radial,
            w_middle,
            w_output,
            w_onsite,
            initial,
        )
    domain = lax.axis_index("dom")
    core = lax.axis_index("sub")
    member = lax.axis_index(("st", "sub"))
    place = jnp.stack([domain, core, member]).astype(jnp.int32)

    own = run_lanes(place, distance.T, neighbours.T, counts.reshape(1, atoms_here))
    own = own + exchange(own, "sub", 1)
    own = own + exchange(own, "st", 1)
    wide = node_feats.astype(F32)
    pack = jnp.concatenate([own.reshape(atoms_here, LANES), wide[:, :LANES], wide[:, LANES:]], axis=0)
    packs = [exchange(pack, "dom", step) for step in range(1, domains)]

    states = jnp.swapaxes(initial, 0, 1)
    half = atoms_here // 2
    part = lax.dynamic_slice_in_dim(states, core * half, half, 1)
    part, packs = lax.optimization_barrier((part, packs))
    left = [exchange(part, "dom", step) for step in range(1, domains)]

    weights = (w_source, w_target, w_radial, w_middle, w_output.T, w_onsite.T)
    pairs = run_network(place, [pack] + packs, weights)
    left, pairs = lax.optimization_barrier((left, pairs))
    right = [exchange(piece, "sub", 1) for piece in left]
    pairs = pairs.reshape(ORB * atoms_all, ORB * LANES)
    alpha_blocks, beta_blocks, last = run_lanczos(place, states, left, right, pairs, float(atoms_all * ORB))
    return (alpha_blocks, beta_blocks, jnp.swapaxes(last, 0, 1))


def solution(mesh):
    placed = (
        P(("grp", "dom"), None),
        P(("grp", "dom"), ("st", "sub")),
        P(("grp", "dom"), ("st", "sub")),
        P(("grp", "dom")),
        P(),
        P(),
        P(),
        P(),
        P(),
        P(),
        P(("grp", "dom"), None, None),
    )
    return jax.shard_map(
        body,
        mesh=mesh,
        in_specs=placed,
        out_specs=(P("grp", None, None), P("grp", None, None), P(("grp", "dom"), None, None)),
        check_vma=False,
    )
```

```python
import jax
import jax.numpy as jnp
from jax import lax
from jax.experimental import pallas as pl
from jax.experimental.pallas import tpu as pltpu
from jax.sharding import PartitionSpec as P

ORB = 13
STEPS = 2


RADIUS = 7.0


def shifted(shard, axis, by):
    devices = lax.axis_size(axis)
    return lax.ppermute(shard, axis, [(i, (i + by) % devices) for i in range(devices)])


def radial(distance, basis_count):
    centres = RADIUS * jnp.arange(basis_count, dtype=jnp.float32) / basis_count
    spacing = RADIUS / basis_count
    return jnp.exp(-jnp.square((distance[..., None] - centres) / (2.0 * spacing)))


def envelope(distance, usable):
    return 0.5 * (jnp.cos(jnp.pi * distance / RADIUS) + 1.0) * usable.astype(jnp.float32)


def onsite_blocks(node_feats, w_onsite):
    projected = jnp.dot(node_feats, w_onsite, preferred_element_type=jnp.float32)
    matrix = projected.reshape(-1, ORB, ORB)
    return (0.5 * (matrix + jnp.swapaxes(matrix, 1, 2))).astype(jnp.bfloat16)


def pair_blocks(source_rows, target_rows, distance, usable, w_radial, w_middle, w_output):
    radial_basis = radial(distance, w_radial.shape[0]).astype(jnp.bfloat16)
    mixed = source_rows[:, None, :].astype(jnp.float32) + target_rows.astype(jnp.float32)
    mixed = mixed + jnp.dot(radial_basis, w_radial, preferred_element_type=jnp.float32)
    hidden_one = jax.nn.silu(mixed).astype(jnp.bfloat16)
    second = jax.nn.silu(jnp.dot(hidden_one, w_middle, preferred_element_type=jnp.float32)).astype(
        jnp.bfloat16
    )
    output_blocks = (
        jnp.dot(second, w_output, preferred_element_type=jnp.float32)
        * envelope(distance, usable)[..., None]
    )
    return output_blocks.astype(jnp.bfloat16).reshape(
        distance.shape[0], distance.shape[1], ORB, ORB
    )


def gram_matrix(left, right, rows_total):
    return jnp.einsum("ris,rit->st", left, right, precision=lax.Precision.HIGHEST) / rows_total


def combine(states, matrix):
    return jnp.einsum("ris,st->rit", states, matrix, precision=lax.Precision.HIGHEST)


def upper_factor(matrix):
    order = matrix.shape[0]
    places = jnp.arange(order, dtype=jnp.int32)

    def column_step(column_index, carry):
        work, lower = carry
        column = lax.dynamic_slice_in_dim(work, column_index, 1, 1)[:, 0]
        pivot = jnp.sqrt(lax.dynamic_slice_in_dim(column, column_index, 1, 0)[0])
        scaled = jnp.where(places >= column_index, column / pivot, jnp.zeros_like(column))
        work = work - scaled[:, None] * scaled[None, :]
        lower = lax.dynamic_update_slice_in_dim(lower, scaled[:, None], column_index, 1)
        return (work, lower)

    work, lower = lax.fori_loop(0, order, column_step, (matrix, jnp.zeros_like(matrix)))
    return lower.T


def upper_inverse(factor):
    order = factor.shape[0]
    identity = jnp.eye(order, dtype=factor.dtype)

    def row_step(counter, inverse):
        row_index = order - 1 - counter
        factor_row = lax.dynamic_slice_in_dim(factor, row_index, 1, 0)
        unit_row = lax.dynamic_slice_in_dim(identity, row_index, 1, 0)
        pivot = lax.dynamic_slice_in_dim(factor_row[0], row_index, 1, 0)[0]
        known = jnp.dot(factor_row, inverse, precision=lax.Precision.HIGHEST)
        fresh = (unit_row - known) / pivot
        return lax.dynamic_update_slice_in_dim(inverse, fresh, row_index, 0)

    return lax.fori_loop(0, order, row_step, jnp.zeros_like(factor))


def divide_right(residue, factor):
    return combine(residue, upper_inverse(factor))


def onsite_apply(onsite, states):
    return jnp.einsum("aij,ajs->ais", onsite, states, precision=lax.Precision.HIGHEST)


def lanczos(states, operate, totals, rows_total):
    factor = upper_factor(totals(gram_matrix(states, states, rows_total)))
    current = divide_right(states, factor)
    previous = current
    beta_prev = factor
    alpha_list = []
    beta_list = []
    for iteration in range(STEPS):
        residue = operate(current)
        if iteration > 0:
            residue = residue - combine(previous, beta_prev.T)
        alpha_block = totals(gram_matrix(current, residue, rows_total))
        residue = residue - combine(current, alpha_block)
        beta_block = upper_factor(totals(gram_matrix(residue, residue, rows_total)))
        previous = current
        current = divide_right(residue, beta_block)
        beta_prev = beta_block
        alpha_list.append(alpha_block)
        beta_list.append(beta_block)
    return (jnp.stack(alpha_list), jnp.stack(beta_list), current)


def body_spread(
    node_feats,
    distance,
    neighbours,
    counts,
    w_source,
    w_target,
    w_radial,
    w_middle,
    w_output,
    w_onsite,
    initial,
):
    atoms_here = node_feats.shape[0]
    slots_here = neighbours.shape[1]
    domain = lax.axis_index("dom")
    member = lax.axis_index(("st", "sub"))
    atoms_all = atoms_here * lax.axis_size("dom")
    rows_total = float(atoms_all * ORB)
    ghost_feats = shifted(node_feats, "dom", -1)
    local_index = (neighbours - domain * atoms_here) % atoms_all
    source = jnp.dot(node_feats, w_source, preferred_element_type=jnp.float32).astype(jnp.bfloat16)
    combined_feats = jnp.concatenate([node_feats, ghost_feats], axis=0)
    target = jnp.dot(combined_feats, w_target, preferred_element_type=jnp.float32).astype(
        jnp.bfloat16
    )
    slot_index = member * slots_here + jnp.arange(slots_here, dtype=jnp.int32)
    usable = slot_index[None, :] < counts[:, None]
    blocks = pair_blocks(
        source, target[local_index], distance, usable, w_radial, w_middle, w_output
    ).astype(jnp.float32)

    def edge_terms(whole_rows, ghost_rows):
        combined = jnp.concatenate([whole_rows, ghost_rows], axis=0)
        forward = jnp.einsum(
            "akij,akjs->ais", blocks, combined[local_index], precision=lax.Precision.HIGHEST
        )
        backward = jnp.einsum("akij,ais->akjs", blocks, whole_rows, precision=lax.Precision.HIGHEST)
        spread = jax.ops.segment_sum(
            backward.reshape(-1, ORB, whole_rows.shape[-1]),
            local_index.reshape(-1),
            num_segments=2 * atoms_here,
        )
        arrived = shifted(spread[atoms_here:], "dom", 1)
        return forward + spread[:atoms_here] + arrived

    onsite = onsite_blocks(node_feats, w_onsite).astype(jnp.float32)

    def operate(current):
        ghost_rows = shifted(current, "dom", -1)
        summed = lax.psum(edge_terms(current, ghost_rows), ("st", "sub"))
        return summed + onsite_apply(onsite, current)

    def totals(value):
        return lax.psum(value, "dom")

    alpha_blocks, beta_blocks, final_rows = lanczos(initial, operate, totals, rows_total)
    return (alpha_blocks, beta_blocks, final_rows)


F32 = jnp.float32
BF16 = jnp.bfloat16
LANES = 128
PAD = 16
PANEL = 8
SKEW = 8
NEAR = 3
VMEM_LIMIT = 56 * 1024 * 1024


def dims(left, right):
    return (((left,), (right,)), ((), ()))


def dot(left, right, contract):
    return lax.dot_general(left, right, contract, preferred_element_type=F32)


def split(value):
    high = value.astype(BF16)
    return high, (value - high.astype(F32)).astype(BF16)


def dot_split(left, right, contract):
    lh, ll = left
    rh, rl = right
    return dot(lh, rh, contract) + (dot(ll, rh, contract) + dot(lh, rl, contract))


NN = dims(1, 0)
NT = dims(1, 1)
TN = dims(0, 0)


def silu(value):
    half = 0.5 * value
    return half + half * jnp.tanh(half)


def spread_rows(value, row, count):
    return jnp.broadcast_to(value[row : row + 1, :], (count, value.shape[1]))


def lanes_kernel(distance, named, counts, out_ref):
    slots, atoms = distance.shape
    member = lax.axis_index(("st", "sub"))
    slot = lax.broadcasted_iota(jnp.int32, (slots, atoms), 0) + member * slots
    usable = slot < counts[...]
    names = jnp.where(usable, named[...], -1).astype(F32)
    turned = jnp.transpose(jnp.concatenate([distance[...], names], axis=0))
    group = atoms // 4
    space = jnp.zeros((2 * group, LANES // 2 - slots), F32)
    for kind in range(2):
        part = turned[:, kind * slots : (kind + 1) * slots]
        first = jnp.concatenate([part[:group], part[2 * group : 3 * group]], axis=0)
        second = jnp.concatenate([part[group : 2 * group], part[3 * group :]], axis=0)
        row = jnp.concatenate([first, space, second, space], axis=1)
        out_ref[kind] = pltpu.roll(row, member * slots, 1)


def run_lanes(distance, named, counts):
    vmem = pl.BlockSpec(memory_space=pltpu.VMEM)
    return pl.pallas_call(
        lanes_kernel,
        out_shape=jax.ShapeDtypeStruct((2, distance.shape[1] // 2, LANES), F32),
        in_specs=[vmem, vmem, vmem],
        out_specs=vmem,
        name="slot_lanes",
    )(distance, named, counts)


def network_kernel(
    pack0,
    pack1,
    pack2,
    pack3,
    w_source,
    w_target,
    w_radial,
    w_middle,
    w_output_t,
    w_onsite_t,
    out_ref,
    pairs,
    envelopes,
    source,
    target,
    onsite,
    feats,
    mixer,
    middle,
    outer,
    raw,
    rows,
    placed_ref,
):
    domain = pl.program_id(0)
    group = pl.program_id(1)
    domains = 4
    groups = pl.num_programs(1)
    atoms = source.shape[1]
    tiles = atoms // 4
    basis = w_radial.shape[0]
    stride = ORB * PAD + SKEW

    @pl.when((domain == 0) & (group == 0))
    def prepare():
        place = lax.axis_index("dom")
        for step, pack in enumerate((pack0, pack1, pack2, pack3)):
            where = place ^ step
            reach = pack[: 2 * tiles]
            pairs[where, 0] = reach
            pairs[where, 1] = pack[2 * tiles : 4 * tiles]
            envelopes[where] = 0.5 * (jnp.cos(jnp.pi * reach / RADIUS) + 1.0)
            got = jnp.concatenate([pack[4 * tiles : 4 * tiles + atoms], pack[4 * tiles + atoms :]], axis=1)
            got = got.astype(BF16)
            source[where] = dot(got, w_source[...], NN)
            target[where] = dot(got, w_target[...], NN)
            feats[where] = got
        empty = jnp.zeros((PAD - ORB, rows.shape[1]), F32)

        def fill_raw(weights):
            for side in range(raw.shape[0]):
                raw[side] = weights[:, side * LANES : (side + 1) * LANES].astype(F32)

        def read_raw(where):
            return jnp.concatenate([raw[side, where, :] for side in range(raw.shape[0])], axis=1)

        def arrange(read):
            for j in range(ORB):
                rows[j * PAD : j * PAD + ORB, :] = read(j)
                rows[j * PAD + ORB : (j + 1) * PAD, :] = empty
            return rows[...].astype(BF16)

        whole = feats[...].reshape(domains * atoms, feats.shape[2])
        fill_raw(w_onsite_t)
        first = dot(arrange(lambda j: read_raw(pl.ds(j, ORB, stride=ORB))), whole, NT)
        second = dot(arrange(lambda j: read_raw(pl.ds(j * ORB, ORB))), whole, NT)
        onsite[...] = 0.5 * (0.5 * (first + second)).astype(BF16).astype(F32)
        fill_raw(w_output_t)
        outer[...] = arrange(lambda j: read_raw(pl.ds(j, ORB, stride=ORB)))

    @pl.when(group == 0)
    def mix():
        following = lax.rem(domain + 1, domains)
        spare = mixer.shape[1] - basis - 3 * atoms
        stacked = jnp.concatenate(
            [
                w_radial[...].astype(F32),
                target[domain],
                target[following],
                source[domain],
                jnp.zeros((spare, mixer.shape[0]), F32),
            ],
            axis=0,
        )
        mixer[...] = stacked.astype(BF16)

    lane = lax.broadcasted_iota(jnp.int32, (1, LANES), 1)
    upper = lane >= LANES // 2
    row2 = lax.broadcasted_iota(jnp.int32, (LANES, LANES), 0)
    column2 = lax.broadcasted_iota(jnp.int32, (LANES, LANES), 1)
    centres = RADIUS * row2.astype(F32) / basis
    scale = 1.0 / (2.0 * RADIUS / basis)
    inputs = []
    envs = []
    names = []
    for u in range(tiles):
        line = pl.ds(group * tiles + u, 1)
        reach = pairs[domain, 0, line, :]
        name = pairs[domain, 1, line, :].astype(jnp.int32)
        envs.append(envelopes[domain, line, :])
        names.append(name)
        radial_t = jnp.exp(-jnp.square((reach - centres) * scale))
        local = lax.rem(name - domain * atoms + domains * atoms, domains * atoms)
        who = group * 2 * tiles + u + jnp.where(upper, tiles, 0)
        near = row2[: 2 * atoms] == local
        mine = row2[: 2 * atoms] == who
        inputs.append(
            jnp.concatenate(
                [radial_t, jnp.where(near, 1.0, 0.0), jnp.where(mine, 1.0, 0.0)], axis=0
            ).astype(BF16)
        )
    columns = jnp.concatenate(inputs, axis=1)
    hidden = silu(dot(columns, mixer[...], TN)).astype(BF16)
    second = silu(dot(hidden, w_middle[...], NN)).astype(BF16)
    blocks = dot(outer[...], second, NT)
    flags = jnp.concatenate(
        [jnp.where(column2 < LANES // 2, row2, -2), jnp.where(column2 < LANES // 2, -2, row2)], axis=0
    )
    for u in range(tiles):
        piece = (blocks[:, u * LANES : (u + 1) * LANES] * envs[u]).astype(BF16)
        chosen = jnp.where(flags == names[u], 1.0, 0.0).astype(BF16)
        placed = dot(piece, chosen, NT)
        for h in range(2):
            place = h * tiles + u
            atom = domain * atoms + group * 2 * tiles + place
            whole = placed[:, h * LANES : (h + 1) * LANES] + jnp.where(lane == atom, onsite[...], 0.0)
            rows_at = slice(place * stride, place * stride + ORB * PAD)
            placed_ref[rows_at, :] = whole
    for j in range(ORB):
        for i in range(ORB):
            tile = placed_ref[pl.ds(j * PAD + i, 2 * tiles, stride=stride), :]
            out_ref[i, :, j * LANES : (j + 1) * LANES] = tile.astype(BF16)


def run_network(packs, weights):
    domains = len(packs)
    atoms = packs[0].shape[0] // 3
    groups = 2
    width = ORB * LANES
    tiles = atoms // 4
    hidden = weights[0].shape[1]
    vmem = pl.BlockSpec(memory_space=pltpu.VMEM)
    return pl.pallas_call(
        network_kernel,
        grid=(domains, groups),
        out_shape=jax.ShapeDtypeStruct((ORB, domains * atoms, width), BF16),
        in_specs=[vmem] * (domains + len(weights)),
        out_specs=pl.BlockSpec((ORB, 2 * tiles, width), lambda d, g: (0, groups * d + g, 0)),
        scratch_shapes=[
            pltpu.VMEM((domains, 2, 2 * tiles, LANES), F32),
            pltpu.VMEM((domains, 2 * tiles, LANES), F32),
            pltpu.VMEM((domains, atoms, hidden), F32),
            pltpu.VMEM((domains, atoms, hidden), F32),
            pltpu.VMEM((ORB * PAD, LANES), F32),
            pltpu.VMEM((domains, atoms, weights[0].shape[0]), BF16),
            pltpu.VMEM((hidden, hidden), BF16),
            pltpu.VMEM((hidden, hidden), BF16),
            pltpu.VMEM((ORB * PAD, hidden), BF16),
            pltpu.VMEM((hidden // LANES, ORB * ORB, LANES), F32),
            pltpu.VMEM((ORB * PAD, hidden), F32),
            pltpu.VMEM((2 * tiles * (ORB * PAD + SKEW), LANES), F32),
        ],
        compiler_params=pltpu.CompilerParams(vmem_limit_bytes=VMEM_LIMIT),
        cost_estimate=pl.CostEstimate(flops=6_000_000_000, bytes_accessed=8_000_000, transcendentals=6_000_000),
        name="pair_network",
    )(*packs, *weights)


def column_of(value, lane):
    return jnp.broadcast_to(value[:, lane : lane + 1], (value.shape[0], LANES))


def split_three(value):
    high = value.astype(BF16)
    rest = value - high.astype(F32)
    middle = rest.astype(BF16)
    return high, middle, (rest - middle.astype(F32)).astype(BF16)


def outer_change(top, side):
    high, middle, low = split_three(top)
    sides = split_three(side)
    wide = [jnp.concatenate([t, s], axis=1) for t, s in zip((high, middle, low), sides)]
    left = jnp.concatenate([high, high, middle, middle, high, low], axis=0)
    right = jnp.concatenate([wide[0], wide[1], wide[0], wide[1], wide[2], wide[0]], axis=0)
    return dot(left, right, TN)


def factor_panels(gram, fill=()):
    order = gram.shape[0]
    count = order // PANEL
    row = lax.broadcasted_iota(jnp.int32, (PANEL, order), 0)
    lane = lax.broadcasted_iota(jnp.int32, (PANEL, order), 1)
    work = [gram[q * PANEL : (q + 1) * PANEL] for q in range(count)]
    extra = [jnp.where(lane == row + q * PANEL, 1.0, 0.0) for q in range(count)]
    upper = []
    inverse = []
    block = [column_of(work[0], k) for k in range(PANEL)]
    for p in range(count):
        base = p * PANEL
        near = [q for q in range(p + 1, min(p + 1 + NEAR, count))]
        beside = {q: [column_of(work[q], base + c) for c in range(PANEL)] for q in near}
        following = [column_of(work[p + 1], base + PANEL + k) for k in range(PANEL)] if near else []
        unit = [jnp.where(row == c, 1.0, 0.0) for c in range(PANEL)]
        roots = jnp.zeros((PANEL, order), F32)
        for r in range(PANEL):
            root = lax.rsqrt(spread_rows(block[r], r, PANEL))
            column = jnp.where(row > r, block[r] * root, 0.0)
            rows = {k: spread_rows(column, k, PANEL) for k in range(r + 1, PANEL)}
            for k in range(r + 1, PANEL):
                block[k] = block[k] - column * rows[k]
            for q in near:
                beside[q][r] = beside[q][r] * root
                for k in range(r + 1, PANEL):
                    beside[q][k] = beside[q][k] - beside[q][r] * rows[k]
            ratio = column * root
            for c in range(r + 1):
                unit[c] = unit[c] - ratio * spread_rows(unit[c], r, PANEL)
            roots = jnp.where(row == r, root, roots)
            if near:
                done = beside[p + 1][r]
                for k in range(PANEL):
                    following[k] = following[k] - done * spread_rows(done, k, PANEL)
        if p < len(fill):
            fill[p]()
        top = unit[0] * spread_rows(work[p], 0, PANEL)
        side = unit[0] * spread_rows(extra[p], 0, PANEL)
        for c in range(1, PANEL):
            top = top + unit[c] * spread_rows(work[p], c, PANEL)
            side = side + unit[c] * spread_rows(extra[p], c, PANEL)
        top = jnp.where(lane >= row + base, top * roots, 0.0)
        side = side * roots
        upper.append(top)
        inverse.append(side)
        if near:
            tops = [spread_rows(top, c, PANEL) for c in range(PANEL)]
            sides = [spread_rows(side, c, PANEL) for c in range(PANEL)]
            for q in near:
                for c in range(PANEL):
                    work[q] = work[q] - beside[q][c] * tops[c]
                    extra[q] = extra[q] - beside[q][c] * sides[c]
            if p + 1 + NEAR < count:
                change = outer_change(top, side)
                for q in range(p + 1 + NEAR, count):
                    rows = slice(q * PANEL, (q + 1) * PANEL)
                    work[q] = work[q] - change[rows, :order]
                    extra[q] = extra[q] - change[rows, order:]
            block = following
    return jnp.concatenate(upper, axis=0), jnp.concatenate(inverse, axis=0)


def lanczos_kernel(
    x_own,
    x_left1,
    x_left2,
    x_left3,
    x_right1,
    x_right2,
    x_right3,
    pairs_hbm,
    alpha_ref,
    beta_ref,
    next_ref,
    pairs,
    xs,
    ys,
    qs,
    flat,
    sem,
    rows_total,
):
    copy = pltpu.make_async_copy(pairs_hbm, pairs, sem)
    copy.start()
    place = lax.axis_index("dom")
    core = lax.axis_index("sub")
    orbitals, atoms, states = x_own.shape
    half = atoms // 2
    total = flat.shape[0]
    scale = 1.0 / rows_total

    def take(source, base):
        xs[:, pl.ds(pl.multiple_of(base, half), source.shape[1]), :] = source[...]

    take(x_own, place * atoms)
    for step, (mine, other) in enumerate(
        ((x_left1, x_right1), (x_left2, x_right2), (x_left3, x_right3)), 1
    ):
        base = (place ^ step) * atoms
        take(mine, base + core * half)
        take(other, base + (1 - core) * half)

    def whole(ref):
        return ref[...].reshape(total, states)

    def own_gram(pieces):
        high, low = pieces
        both = dot(high, jnp.concatenate([high, low], axis=1), TN)
        cross = both[:, states:]
        return (both[:, :states] + (cross + jnp.transpose(cross))) * scale

    def set_flat(pieces):
        flat[:, :states] = pieces[0]
        flat[:, states:] = pieces[1]

    chunk = 208
    width = 256

    def forward(start):
        def run():
            both = dot(pairs[start : start + chunk, :], flat[...], NN)
            ys[start : start + chunk, :] = both[:, :states] + both[:, states:]

        return run

    def backward(start):
        stop = min(start + width, total)

        def run():
            both = dot(pairs[:, start:stop], flat[...], TN)
            ys[start:stop, :] = ys[start:stop, :] + (both[:, :states] + both[:, states:])

        return run

    fill = [forward(start) for start in range(0, total, chunk)]
    fill = fill + [backward(start) for start in range(0, total, width)]

    def side(pieces):
        return jnp.concatenate(pieces, axis=1)

    def fold(both):
        return both[:, :states] + both[:, states:]

    def times(left, right):
        return fold(dot(left, jnp.concatenate([side(right), side(right)], axis=0), NN))

    def times_turned(left, right):
        high, low = right
        wide = jnp.concatenate([side((high, high)), side((low, low))], axis=0)
        return fold(dot(left, wide, NT))

    def overlap(left, right):
        both = fold(dot(left, right, TN))
        return (both[:states] + both[states:]) * scale

    pieces = split(whole(xs))
    set_flat(pieces)
    gram = own_gram(pieces)
    copy.wait()
    factor, inverse = factor_panels(gram, fill)
    inverse = split(inverse)
    first = side(split(times_turned(flat[...], inverse)))
    qs[...] = first
    residue = times_turned(side(split(ys[...])), inverse)
    alpha = overlap(first, side(split(residue)))
    alpha_ref[0] = alpha
    residue = residue - times(first, split(alpha))
    pieces = split(residue)
    set_flat(pieces)
    gram = own_gram(pieces)
    factor, inverse = factor_panels(gram, fill)
    beta_ref[0] = factor
    inverse = split(inverse)
    first = side(split(times_turned(flat[...], inverse)))
    residue = times_turned(side(split(ys[...])), inverse) - times_turned(qs[...], split(factor))
    alpha = overlap(first, side(split(residue)))
    alpha_ref[1] = alpha
    residue = residue - times(first, split(alpha))
    xs[...] = residue.reshape(xs.shape)
    gram = own_gram(split(residue))
    factor, inverse = factor_panels(gram)
    beta_ref[1] = factor
    mine = xs[:, pl.ds(pl.multiple_of(place * atoms, atoms), atoms), :].reshape(orbitals * atoms, states)
    mine = times_turned(side(split(mine)), split(inverse))
    next_ref[...] = mine.reshape(orbitals, atoms, states)


def run_lanczos(own, left, right, pairs, rows_total):
    states = own.shape[2]
    total = pairs.shape[0]
    vmem = pl.BlockSpec(memory_space=pltpu.VMEM)

    def kernel(*refs):
        lanczos_kernel(*refs, rows_total)

    return pl.pallas_call(
        kernel,
        out_shape=(
            jax.ShapeDtypeStruct((STEPS, states, states), F32),
            jax.ShapeDtypeStruct((STEPS, states, states), F32),
            jax.ShapeDtypeStruct(own.shape, F32),
        ),
        in_specs=[vmem] * 7 + [pl.BlockSpec(memory_space=pl.ANY)],
        out_specs=(vmem, vmem, vmem),
        scratch_shapes=[
            pltpu.VMEM(pairs.shape, BF16),
            pltpu.VMEM((own.shape[0], total // own.shape[0], states), F32),
            pltpu.VMEM((total, states), F32),
            pltpu.VMEM((total, 2 * states), BF16),
            pltpu.VMEM((total, 2 * states), BF16),
            pltpu.SemaphoreType.DMA,
        ],
        compiler_params=pltpu.CompilerParams(vmem_limit_bytes=VMEM_LIMIT),
        name="block_lanczos",
    )(own, *left, *right, pairs)


def exchange(shard, axis, mask):
    devices = lax.axis_size(axis)
    return lax.ppermute(shard, axis, [(i, i ^ mask) for i in range(devices)])


def body(
    node_feats,
    distance,
    neighbours,
    counts,
    w_source,
    w_target,
    w_radial,
    w_middle,
    w_output,
    w_onsite,
    initial,
):
    atoms_here, slots_here = neighbours.shape
    domains = lax.axis_size("dom")
    members = lax.axis_size("st") * lax.axis_size("sub")
    atoms_all = atoms_here * domains
    suits = (domains, atoms_all, 2 * members * slots_here, initial.shape[2]) == (4, LANES, LANES, LANES)
    if not (suits and lax.axis_size("sub") == 2 and lax.axis_size("st") == 2):
        return body_spread(
            node_feats,
            distance,
            neighbours,
            counts,
            w_source,
            w_target,
            w_radial,
            w_middle,
            w_output,
            w_onsite,
            initial,
        )
    domain = lax.axis_index("dom")
    core = lax.axis_index("sub")
    member = lax.axis_index(("st", "sub"))

    own = run_lanes(distance.T, neighbours.T, counts.reshape(1, atoms_here))
    states = jnp.swapaxes(initial, 0, 1)
    half = atoms_here // 2
    part = lax.dynamic_slice_in_dim(states, core * half, half, 1)
    left = [exchange(part, "dom", step) for step in range(1, domains)]
    own = own + exchange(own, "sub", 1)
    own = own + exchange(own, "st", 1)
    wide = node_feats.astype(F32)
    pack = jnp.concatenate([own.reshape(atoms_here, LANES), wide[:, :LANES], wide[:, LANES:]], axis=0)
    packs = [exchange(pack, "dom", 1), exchange(pack, "dom", 2)]
    packs = packs + [exchange(packs[0], "dom", 2)]


    weights = (w_source, w_target, w_radial, w_middle, w_output.T, w_onsite.T)
    packs, left = lax.optimization_barrier((packs, left))
    right = [exchange(piece, "sub", 1) for piece in left]
    pairs = run_network([pack] + packs, weights)
    pairs = pairs.reshape(ORB * atoms_all, ORB * LANES)
    alpha_blocks, beta_blocks, last = run_lanczos(states, left, right, pairs, float(atoms_all * ORB))
    return (alpha_blocks, beta_blocks, jnp.swapaxes(last, 0, 1))


def solution(mesh):
    placed = (
        P(("grp", "dom"), None),
        P(("grp", "dom"), ("st", "sub")),
        P(("grp", "dom"), ("st", "sub")),
        P(("grp", "dom")),
        P(),
        P(),
        P(),
        P(),
        P(),
        P(),
        P(("grp", "dom"), None, None),
    )
    return jax.shard_map(
        body,
        mesh=mesh,
        in_specs=placed,
        out_specs=(P("grp", None, None), P("grp", None, None), P(("grp", "dom"), None, None)),
        check_vma=False,
    )
```

```python
import jax
import jax.numpy as jnp
from jax import lax
from jax.experimental import pallas as pl
from jax.experimental.pallas import tpu as pltpu
from jax.sharding import PartitionSpec as P

ORB = 13
STEPS = 2


RADIUS = 7.0


def shifted(shard, axis, by):
    devices = lax.axis_size(axis)
    return lax.ppermute(shard, axis, [(i, (i + by) % devices) for i in range(devices)])


def radial(distance, basis_count):
    centres = RADIUS * jnp.arange(basis_count, dtype=jnp.float32) / basis_count
    spacing = RADIUS / basis_count
    return jnp.exp(-jnp.square((distance[..., None] - centres) / (2.0 * spacing)))


def envelope(distance, usable):
    return 0.5 * (jnp.cos(jnp.pi * distance / RADIUS) + 1.0) * usable.astype(jnp.float32)


def onsite_blocks(node_feats, w_onsite):
    projected = jnp.dot(node_feats, w_onsite, preferred_element_type=jnp.float32)
    matrix = projected.reshape(-1, ORB, ORB)
    return (0.5 * (matrix + jnp.swapaxes(matrix, 1, 2))).astype(jnp.bfloat16)


def pair_blocks(source_rows, target_rows, distance, usable, w_radial, w_middle, w_output):
    radial_basis = radial(distance, w_radial.shape[0]).astype(jnp.bfloat16)
    mixed = source_rows[:, None, :].astype(jnp.float32) + target_rows.astype(jnp.float32)
    mixed = mixed + jnp.dot(radial_basis, w_radial, preferred_element_type=jnp.float32)
    hidden_one = jax.nn.silu(mixed).astype(jnp.bfloat16)
    second = jax.nn.silu(jnp.dot(hidden_one, w_middle, preferred_element_type=jnp.float32)).astype(
        jnp.bfloat16
    )
    output_blocks = (
        jnp.dot(second, w_output, preferred_element_type=jnp.float32)
        * envelope(distance, usable)[..., None]
    )
    return output_blocks.astype(jnp.bfloat16).reshape(
        distance.shape[0], distance.shape[1], ORB, ORB
    )


def gram_matrix(left, right, rows_total):
    return jnp.einsum("ris,rit->st", left, right, precision=lax.Precision.HIGHEST) / rows_total


def combine(states, matrix):
    return jnp.einsum("ris,st->rit", states, matrix, precision=lax.Precision.HIGHEST)


def upper_factor(matrix):
    order = matrix.shape[0]
    places = jnp.arange(order, dtype=jnp.int32)

    def column_step(column_index, carry):
        work, lower = carry
        column = lax.dynamic_slice_in_dim(work, column_index, 1, 1)[:, 0]
        pivot = jnp.sqrt(lax.dynamic_slice_in_dim(column, column_index, 1, 0)[0])
        scaled = jnp.where(places >= column_index, column / pivot, jnp.zeros_like(column))
        work = work - scaled[:, None] * scaled[None, :]
        lower = lax.dynamic_update_slice_in_dim(lower, scaled[:, None], column_index, 1)
        return (work, lower)

    work, lower = lax.fori_loop(0, order, column_step, (matrix, jnp.zeros_like(matrix)))
    return lower.T


def upper_inverse(factor):
    order = factor.shape[0]
    identity = jnp.eye(order, dtype=factor.dtype)

    def row_step(counter, inverse):
        row_index = order - 1 - counter
        factor_row = lax.dynamic_slice_in_dim(factor, row_index, 1, 0)
        unit_row = lax.dynamic_slice_in_dim(identity, row_index, 1, 0)
        pivot = lax.dynamic_slice_in_dim(factor_row[0], row_index, 1, 0)[0]
        known = jnp.dot(factor_row, inverse, precision=lax.Precision.HIGHEST)
        fresh = (unit_row - known) / pivot
        return lax.dynamic_update_slice_in_dim(inverse, fresh, row_index, 0)

    return lax.fori_loop(0, order, row_step, jnp.zeros_like(factor))


def divide_right(residue, factor):
    return combine(residue, upper_inverse(factor))


def onsite_apply(onsite, states):
    return jnp.einsum("aij,ajs->ais", onsite, states, precision=lax.Precision.HIGHEST)


def lanczos(states, operate, totals, rows_total):
    factor = upper_factor(totals(gram_matrix(states, states, rows_total)))
    current = divide_right(states, factor)
    previous = current
    beta_prev = factor
    alpha_list = []
    beta_list = []
    for iteration in range(STEPS):
        residue = operate(current)
        if iteration > 0:
            residue = residue - combine(previous, beta_prev.T)
        alpha_block = totals(gram_matrix(current, residue, rows_total))
        residue = residue - combine(current, alpha_block)
        beta_block = upper_factor(totals(gram_matrix(residue, residue, rows_total)))
        previous = current
        current = divide_right(residue, beta_block)
        beta_prev = beta_block
        alpha_list.append(alpha_block)
        beta_list.append(beta_block)
    return (jnp.stack(alpha_list), jnp.stack(beta_list), current)


def body_spread(
    node_feats,
    distance,
    neighbours,
    counts,
    w_source,
    w_target,
    w_radial,
    w_middle,
    w_output,
    w_onsite,
    initial,
):
    atoms_here = node_feats.shape[0]
    slots_here = neighbours.shape[1]
    domain = lax.axis_index("dom")
    member = lax.axis_index(("st", "sub"))
    atoms_all = atoms_here * lax.axis_size("dom")
    rows_total = float(atoms_all * ORB)
    ghost_feats = shifted(node_feats, "dom", -1)
    local_index = (neighbours - domain * atoms_here) % atoms_all
    source = jnp.dot(node_feats, w_source, preferred_element_type=jnp.float32).astype(jnp.bfloat16)
    combined_feats = jnp.concatenate([node_feats, ghost_feats], axis=0)
    target = jnp.dot(combined_feats, w_target, preferred_element_type=jnp.float32).astype(
        jnp.bfloat16
    )
    slot_index = member * slots_here + jnp.arange(slots_here, dtype=jnp.int32)
    usable = slot_index[None, :] < counts[:, None]
    blocks = pair_blocks(
        source, target[local_index], distance, usable, w_radial, w_middle, w_output
    ).astype(jnp.float32)

    def edge_terms(whole_rows, ghost_rows):
        combined = jnp.concatenate([whole_rows, ghost_rows], axis=0)
        forward = jnp.einsum(
            "akij,akjs->ais", blocks, combined[local_index], precision=lax.Precision.HIGHEST
        )
        backward = jnp.einsum("akij,ais->akjs", blocks, whole_rows, precision=lax.Precision.HIGHEST)
        spread = jax.ops.segment_sum(
            backward.reshape(-1, ORB, whole_rows.shape[-1]),
            local_index.reshape(-1),
            num_segments=2 * atoms_here,
        )
        arrived = shifted(spread[atoms_here:], "dom", 1)
        return forward + spread[:atoms_here] + arrived

    onsite = onsite_blocks(node_feats, w_onsite).astype(jnp.float32)

    def operate(current):
        ghost_rows = shifted(current, "dom", -1)
        summed = lax.psum(edge_terms(current, ghost_rows), ("st", "sub"))
        return summed + onsite_apply(onsite, current)

    def totals(value):
        return lax.psum(value, "dom")

    alpha_blocks, beta_blocks, final_rows = lanczos(initial, operate, totals, rows_total)
    return (alpha_blocks, beta_blocks, final_rows)


F32 = jnp.float32
BF16 = jnp.bfloat16
LANES = 128
PAD = 16
PANEL = 8
SKEW = 8
NEAR = 3
VMEM_LIMIT = 56 * 1024 * 1024


def dims(left, right):
    return (((left,), (right,)), ((), ()))


def dot(left, right, contract):
    return lax.dot_general(left, right, contract, preferred_element_type=F32)


def split(value):
    high = value.astype(BF16)
    return high, (value - high.astype(F32)).astype(BF16)


def dot_split(left, right, contract):
    lh, ll = left
    rh, rl = right
    return dot(lh, rh, contract) + (dot(ll, rh, contract) + dot(lh, rl, contract))


NN = dims(1, 0)
NT = dims(1, 1)
TN = dims(0, 0)


def silu(value):
    half = 0.5 * value
    return half + half * jnp.tanh(half)


def spread_rows(value, row, count):
    return jnp.broadcast_to(value[row : row + 1, :], (count, value.shape[1]))


def lanes_kernel(distance, named, counts, out_ref):
    slots, atoms = distance.shape
    member = lax.axis_index(("st", "sub"))
    slot = lax.broadcasted_iota(jnp.int32, (slots, atoms), 0) + member * slots
    usable = slot < counts[...]
    names = jnp.where(usable, named[...], -1).astype(F32)
    turned = jnp.transpose(jnp.concatenate([distance[...], names], axis=0))
    group = atoms // 4
    space = jnp.zeros((2 * group, LANES // 2 - slots), F32)
    for kind in range(2):
        part = turned[:, kind * slots : (kind + 1) * slots]
        first = jnp.concatenate([part[:group], part[2 * group : 3 * group]], axis=0)
        second = jnp.concatenate([part[group : 2 * group], part[3 * group :]], axis=0)
        row = jnp.concatenate([first, space, second, space], axis=1)
        out_ref[kind] = pltpu.roll(row, member * slots, 1)


def run_lanes(distance, named, counts):
    vmem = pl.BlockSpec(memory_space=pltpu.VMEM)
    return pl.pallas_call(
        lanes_kernel,
        out_shape=jax.ShapeDtypeStruct((2, distance.shape[1] // 2, LANES), F32),
        in_specs=[vmem, vmem, vmem],
        out_specs=vmem,
        name="slot_lanes",
    )(distance, named, counts)


def network_kernel(
    pack0,
    pack1,
    pack2,
    pack3,
    w_source,
    w_target,
    w_radial,
    w_middle,
    w_output_t,
    w_onsite_t,
    out_ref,
    pairs,
    envelopes,
    source,
    target,
    onsite,
    feats,
    mixer,
    middle,
    outer,
    raw,
    rows,
    placed_ref,
):
    domain = pl.program_id(0)
    group = pl.program_id(1)
    domains = 4
    groups = pl.num_programs(1)
    atoms = source.shape[1]
    tiles = atoms // 4
    basis = w_radial.shape[0]
    stride = ORB * PAD + SKEW

    @pl.when((domain == 0) & (group == 0))
    def prepare():
        place = lax.axis_index("dom")
        for step, pack in enumerate((pack0, pack1, pack2, pack3)):
            where = place ^ step
            reach = pack[: 2 * tiles]
            pairs[where, 0] = reach
            pairs[where, 1] = pack[2 * tiles : 4 * tiles]
            envelopes[where] = 0.5 * (jnp.cos(jnp.pi * reach / RADIUS) + 1.0)
            got = jnp.concatenate([pack[4 * tiles : 4 * tiles + atoms], pack[4 * tiles + atoms :]], axis=1)
            got = got.astype(BF16)
            source[where] = dot(got, w_source[...], NN)
            target[where] = dot(got, w_target[...], NN)
            feats[where] = got
        empty = jnp.zeros((PAD - ORB, rows.shape[1]), F32)

        def fill_raw(weights):
            for side in range(raw.shape[0]):
                raw[side] = weights[:, side * LANES : (side + 1) * LANES].astype(F32)

        def read_raw(where):
            return jnp.concatenate([raw[side, where, :] for side in range(raw.shape[0])], axis=1)

        def arrange(read):
            for j in range(ORB):
                rows[j * PAD : j * PAD + ORB, :] = read(j)
                rows[j * PAD + ORB : (j + 1) * PAD, :] = empty
            return rows[...].astype(BF16)

        whole = feats[...].reshape(domains * atoms, feats.shape[2])
        fill_raw(w_onsite_t)
        first = dot(arrange(lambda j: read_raw(pl.ds(j, ORB, stride=ORB))), whole, NT)
        second = dot(arrange(lambda j: read_raw(pl.ds(j * ORB, ORB))), whole, NT)
        onsite[...] = 0.5 * (0.5 * (first + second)).astype(BF16).astype(F32)
        fill_raw(w_output_t)
        outer[...] = arrange(lambda j: read_raw(pl.ds(j, ORB, stride=ORB)))

    @pl.when(group == 0)
    def mix():
        following = lax.rem(domain + 1, domains)
        spare = mixer.shape[1] - basis - 3 * atoms
        stacked = jnp.concatenate(
            [
                w_radial[...].astype(F32),
                target[domain],
                target[following],
                source[domain],
                jnp.zeros((spare, mixer.shape[0]), F32),
            ],
            axis=0,
        )
        mixer[...] = stacked.astype(BF16)

    lane = lax.broadcasted_iota(jnp.int32, (1, LANES), 1)
    upper = lane >= LANES // 2
    row2 = lax.broadcasted_iota(jnp.int32, (LANES, LANES), 0)
    column2 = lax.broadcasted_iota(jnp.int32, (LANES, LANES), 1)
    centres = RADIUS * row2.astype(F32) / basis
    scale = 1.0 / (2.0 * RADIUS / basis)
    inputs = []
    envs = []
    names = []
    for u in range(tiles):
        line = pl.ds(group * tiles + u, 1)
        reach = pairs[domain, 0, line, :]
        name = pairs[domain, 1, line, :].astype(jnp.int32)
        envs.append(envelopes[domain, line, :])
        names.append(name)
        radial_t = jnp.exp(-jnp.square((reach - centres) * scale))
        local = lax.rem(name - domain * atoms + domains * atoms, domains * atoms)
        who = group * 2 * tiles + u + jnp.where(upper, tiles, 0)
        near = row2[: 2 * atoms] == local
        mine = row2[: 2 * atoms] == who
        inputs.append(
            jnp.concatenate(
                [radial_t, jnp.where(near, 1.0, 0.0), jnp.where(mine, 1.0, 0.0)], axis=0
            ).astype(BF16)
        )
    columns = jnp.concatenate(inputs, axis=1)
    hidden = silu(dot(columns, mixer[...], TN)).astype(BF16)
    second = silu(dot(hidden, w_middle[...], NN)).astype(BF16)
    blocks = dot(outer[...], second, NT)
    flags = jnp.concatenate(
        [jnp.where(column2 < LANES // 2, row2, -2), jnp.where(column2 < LANES // 2, -2, row2)], axis=0
    )
    for u in range(tiles):
        piece = (blocks[:, u * LANES : (u + 1) * LANES] * envs[u]).astype(BF16)
        chosen = jnp.where(flags == names[u], 1.0, 0.0).astype(BF16)
        placed = dot(piece, chosen, NT)
        for h in range(2):
            place = h * tiles + u
            atom = domain * atoms + group * 2 * tiles + place
            whole = placed[:, h * LANES : (h + 1) * LANES] + jnp.where(lane == atom, onsite[...], 0.0)
            rows_at = slice(place * stride, place * stride + ORB * PAD)
            placed_ref[rows_at, :] = whole
    for j in range(ORB):
        for i in range(ORB):
            tile = placed_ref[pl.ds(j * PAD + i, 2 * tiles, stride=stride), :]
            out_ref[i, :, j * LANES : (j + 1) * LANES] = tile.astype(BF16)


def run_network(packs, weights):
    domains = len(packs)
    atoms = packs[0].shape[0] // 3
    groups = 2
    width = ORB * LANES
    tiles = atoms // 4
    hidden = weights[0].shape[1]
    vmem = pl.BlockSpec(memory_space=pltpu.VMEM)
    return pl.pallas_call(
        network_kernel,
        grid=(domains, groups),
        out_shape=jax.ShapeDtypeStruct((ORB, domains * atoms, width), BF16),
        in_specs=[vmem] * (domains + len(weights)),
        out_specs=pl.BlockSpec((ORB, 2 * tiles, width), lambda d, g: (0, groups * d + g, 0)),
        scratch_shapes=[
            pltpu.VMEM((domains, 2, 2 * tiles, LANES), F32),
            pltpu.VMEM((domains, 2 * tiles, LANES), F32),
            pltpu.VMEM((domains, atoms, hidden), F32),
            pltpu.VMEM((domains, atoms, hidden), F32),
            pltpu.VMEM((ORB * PAD, LANES), F32),
            pltpu.VMEM((domains, atoms, weights[0].shape[0]), BF16),
            pltpu.VMEM((hidden, hidden), BF16),
            pltpu.VMEM((hidden, hidden), BF16),
            pltpu.VMEM((ORB * PAD, hidden), BF16),
            pltpu.VMEM((hidden // LANES, ORB * ORB, LANES), F32),
            pltpu.VMEM((ORB * PAD, hidden), F32),
            pltpu.VMEM((2 * tiles * (ORB * PAD + SKEW), LANES), F32),
        ],
        compiler_params=pltpu.CompilerParams(vmem_limit_bytes=VMEM_LIMIT),
        cost_estimate=pl.CostEstimate(flops=6_000_000_000, bytes_accessed=8_000_000, transcendentals=6_000_000),
        name="pair_network",
    )(*packs, *weights)


def column_of(value, lane):
    return jnp.broadcast_to(value[:, lane : lane + 1], (value.shape[0], LANES))


def split_three(value):
    high = value.astype(BF16)
    rest = value - high.astype(F32)
    middle = rest.astype(BF16)
    return high, middle, (rest - middle.astype(F32)).astype(BF16)


def outer_change(top, side):
    high, middle, low = split_three(top)
    sides = split_three(side)
    wide = [jnp.concatenate([t, s], axis=1) for t, s in zip((high, middle, low), sides)]
    left = jnp.concatenate([high, high, middle, middle, high, low], axis=0)
    right = jnp.concatenate([wide[0], wide[1], wide[0], wide[1], wide[2], wide[0]], axis=0)
    return dot(left, right, TN)


def factor_panels(gram, fill=()):
    order = gram.shape[0]
    count = order // PANEL
    row = lax.broadcasted_iota(jnp.int32, (PANEL, order), 0)
    lane = lax.broadcasted_iota(jnp.int32, (PANEL, order), 1)
    work = [gram[q * PANEL : (q + 1) * PANEL] for q in range(count)]
    extra = [jnp.where(lane == row + q * PANEL, 1.0, 0.0) for q in range(count)]
    upper = []
    inverse = []
    block = [column_of(work[0], k) for k in range(PANEL)]
    for p in range(count):
        base = p * PANEL
        near = [q for q in range(p + 1, min(p + 1 + NEAR, count))]
        beside = {q: [column_of(work[q], base + c) for c in range(PANEL)] for q in near}
        following = [column_of(work[p + 1], base + PANEL + k) for k in range(PANEL)] if near else []
        unit = [jnp.where(row == c, 1.0, 0.0) for c in range(PANEL)]
        roots = jnp.zeros((PANEL, order), F32)
        for r in range(PANEL):
            root = lax.rsqrt(spread_rows(block[r], r, PANEL))
            column = jnp.where(row > r, block[r] * root, 0.0)
            rows = {k: spread_rows(column, k, PANEL) for k in range(r + 1, PANEL)}
            for k in range(r + 1, PANEL):
                block[k] = block[k] - column * rows[k]
            for q in near:
                beside[q][r] = beside[q][r] * root
                for k in range(r + 1, PANEL):
                    beside[q][k] = beside[q][k] - beside[q][r] * rows[k]
            ratio = column * root
            for c in range(r + 1):
                unit[c] = unit[c] - ratio * spread_rows(unit[c], r, PANEL)
            roots = jnp.where(row == r, root, roots)
            if near:
                done = beside[p + 1][r]
                for k in range(PANEL):
                    following[k] = following[k] - done * spread_rows(done, k, PANEL)
        top = unit[0] * spread_rows(work[p], 0, PANEL)
        side = unit[0] * spread_rows(extra[p], 0, PANEL)
        for c in range(1, PANEL):
            top = top + unit[c] * spread_rows(work[p], c, PANEL)
            side = side + unit[c] * spread_rows(extra[p], c, PANEL)
        top = jnp.where(lane >= row + base, top * roots, 0.0)
        side = side * roots
        upper.append(top)
        inverse.append(side)
        if near:
            tops = [spread_rows(top, c, PANEL) for c in range(PANEL)]
            sides = [spread_rows(side, c, PANEL) for c in range(PANEL)]
            for q in near:
                for c in range(PANEL):
                    work[q] = work[q] - beside[q][c] * tops[c]
                    extra[q] = extra[q] - beside[q][c] * sides[c]
            if p + 1 + NEAR < count:
                change = outer_change(top, side)
                if p < len(fill):
                    fill[p]()
                for q in range(p + 1 + NEAR, count):
                    rows = slice(q * PANEL, (q + 1) * PANEL)
                    work[q] = work[q] - change[rows, :order]
                    extra[q] = extra[q] - change[rows, order:]
            block = following
    for run in fill[count - 1 - NEAR :]:
        run()
    return jnp.concatenate(upper, axis=0), jnp.concatenate(inverse, axis=0)


def lanczos_kernel(
    x_own,
    x_left1,
    x_left2,
    x_left3,
    x_right1,
    x_right2,
    x_right3,
    pairs_hbm,
    alpha_ref,
    beta_ref,
    next_ref,
    pairs,
    xs,
    ys,
    qs,
    flat,
    sem,
    rows_total,
):
    copy = pltpu.make_async_copy(pairs_hbm, pairs, sem)
    copy.start()
    place = lax.axis_index("dom")
    core = lax.axis_index("sub")
    orbitals, atoms, states = x_own.shape
    half = atoms // 2
    total = flat.shape[0]
    scale = 1.0 / rows_total

    def take(source, base):
        xs[:, pl.ds(pl.multiple_of(base, half), source.shape[1]), :] = source[...]

    take(x_own, place * atoms)
    for step, (mine, other) in enumerate(
        ((x_left1, x_right1), (x_left2, x_right2), (x_left3, x_right3)), 1
    ):
        base = (place ^ step) * atoms
        take(mine, base + core * half)
        take(other, base + (1 - core) * half)

    def whole(ref):
        return ref[...].reshape(total, states)

    def own_gram(pieces):
        high, low = pieces
        both = dot(high, jnp.concatenate([high, low], axis=1), TN)
        cross = both[:, states:]
        return (both[:, :states] + (cross + jnp.transpose(cross))) * scale

    def set_flat(pieces):
        flat[:, :states] = pieces[0]
        flat[:, states:] = pieces[1]

    chunk = 416
    width = 512

    def forward(start):
        def run():
            both = dot(pairs[start : start + chunk, :], flat[...], NN)
            ys[start : start + chunk, :] = both[:, :states] + both[:, states:]

        return run

    def backward(start):
        stop = min(start + width, total)

        def run():
            both = dot(pairs[:, start:stop], flat[...], TN)
            ys[start:stop, :] = ys[start:stop, :] + (both[:, :states] + both[:, states:])

        return run

    fill = [forward(start) for start in range(0, total, chunk)]
    fill = fill + [backward(start) for start in range(0, total, width)]

    def side(pieces):
        return jnp.concatenate(pieces, axis=1)

    def fold(both):
        return both[:, :states] + both[:, states:]

    def times(left, right):
        return fold(dot(left, jnp.concatenate([side(right), side(right)], axis=0), NN))

    def times_turned(left, right):
        high, low = right
        wide = jnp.concatenate([side((high, high)), side((low, low))], axis=0)
        return fold(dot(left, wide, NT))

    def overlap(left, right):
        both = fold(dot(left, right, TN))
        return (both[:states] + both[states:]) * scale

    pieces = split(whole(xs))
    set_flat(pieces)
    gram = own_gram(pieces)
    factor, inverse = factor_panels(gram)
    copy.wait()
    for run in fill:
        run()
    inverse = split(inverse)
    first = side(split(times_turned(flat[...], inverse)))
    qs[...] = first
    residue = times_turned(side(split(ys[...])), inverse)
    alpha = overlap(first, side(split(residue)))
    alpha_ref[0] = alpha
    residue = residue - times(first, split(alpha))
    pieces = split(residue)
    set_flat(pieces)
    gram = own_gram(pieces)
    factor, inverse = factor_panels(gram, fill)
    beta_ref[0] = factor
    inverse = split(inverse)
    first = side(split(times_turned(flat[...], inverse)))
    residue = times_turned(side(split(ys[...])), inverse) - times_turned(qs[...], split(factor))
    alpha = overlap(first, side(split(residue)))
    alpha_ref[1] = alpha
    residue = residue - times(first, split(alpha))
    xs[...] = residue.reshape(xs.shape)
    gram = own_gram(split(residue))
    factor, inverse = factor_panels(gram)
    beta_ref[1] = factor
    mine = xs[:, pl.ds(pl.multiple_of(place * atoms, atoms), atoms), :].reshape(orbitals * atoms, states)
    mine = times_turned(side(split(mine)), split(inverse))
    next_ref[...] = mine.reshape(orbitals, atoms, states)


def run_lanczos(own, left, right, pairs, rows_total):
    states = own.shape[2]
    total = pairs.shape[0]
    vmem = pl.BlockSpec(memory_space=pltpu.VMEM)

    def kernel(*refs):
        lanczos_kernel(*refs, rows_total)

    return pl.pallas_call(
        kernel,
        out_shape=(
            jax.ShapeDtypeStruct((STEPS, states, states), F32),
            jax.ShapeDtypeStruct((STEPS, states, states), F32),
            jax.ShapeDtypeStruct(own.shape, F32),
        ),
        in_specs=[vmem] * 7 + [pl.BlockSpec(memory_space=pl.ANY)],
        out_specs=(vmem, vmem, vmem),
        scratch_shapes=[
            pltpu.VMEM(pairs.shape, BF16),
            pltpu.VMEM((own.shape[0], total // own.shape[0], states), F32),
            pltpu.VMEM((total, states), F32),
            pltpu.VMEM((total, 2 * states), BF16),
            pltpu.VMEM((total, 2 * states), BF16),
            pltpu.SemaphoreType.DMA,
        ],
        compiler_params=pltpu.CompilerParams(vmem_limit_bytes=VMEM_LIMIT),
        name="block_lanczos",
    )(own, *left, *right, pairs)


def exchange(shard, axis, mask):
    devices = lax.axis_size(axis)
    return lax.ppermute(shard, axis, [(i, i ^ mask) for i in range(devices)])


def body(
    node_feats,
    distance,
    neighbours,
    counts,
    w_source,
    w_target,
    w_radial,
    w_middle,
    w_output,
    w_onsite,
    initial,
):
    atoms_here, slots_here = neighbours.shape
    domains = lax.axis_size("dom")
    members = lax.axis_size("st") * lax.axis_size("sub")
    atoms_all = atoms_here * domains
    suits = (domains, atoms_all, 2 * members * slots_here, initial.shape[2]) == (4, LANES, LANES, LANES)
    if not (suits and lax.axis_size("sub") == 2 and lax.axis_size("st") == 2):
        return body_spread(
            node_feats,
            distance,
            neighbours,
            counts,
            w_source,
            w_target,
            w_radial,
            w_middle,
            w_output,
            w_onsite,
            initial,
        )
    domain = lax.axis_index("dom")
    core = lax.axis_index("sub")
    member = lax.axis_index(("st", "sub"))

    own = run_lanes(distance.T, neighbours.T, counts.reshape(1, atoms_here))
    states = jnp.swapaxes(initial, 0, 1)
    half = atoms_here // 2
    part = lax.dynamic_slice_in_dim(states, core * half, half, 1)
    left = [exchange(part, "dom", step) for step in range(1, domains)]
    own = own + exchange(own, "sub", 1)
    own = own + exchange(own, "st", 1)
    wide = node_feats.astype(F32)
    pack = jnp.concatenate([own.reshape(atoms_here, LANES), wide[:, :LANES], wide[:, LANES:]], axis=0)
    packs = [exchange(pack, "dom", 1), exchange(pack, "dom", 2)]
    packs = packs + [exchange(packs[0], "dom", 2)]


    weights = (w_source, w_target, w_radial, w_middle, w_output.T, w_onsite.T)
    packs, left = lax.optimization_barrier((packs, left))
    right = [exchange(piece, "sub", 1) for piece in left]
    pairs = run_network([pack] + packs, weights)
    pairs = pairs.reshape(ORB * atoms_all, ORB * LANES)
    alpha_blocks, beta_blocks, last = run_lanczos(states, left, right, pairs, float(atoms_all * ORB))
    return (alpha_blocks, beta_blocks, jnp.swapaxes(last, 0, 1))


def solution(mesh):
    placed = (
        P(("grp", "dom"), None),
        P(("grp", "dom"), ("st", "sub")),
        P(("grp", "dom"), ("st", "sub")),
        P(("grp", "dom")),
        P(),
        P(),
        P(),
        P(),
        P(),
        P(),
        P(("grp", "dom"), None, None),
    )
    return jax.shard_map(
        body,
        mesh=mesh,
        in_specs=placed,
        out_specs=(P("grp", None, None), P("grp", None, None), P(("grp", "dom"), None, None)),
        check_vma=False,
    )
```
